256 devices in a mesh: row: 16 (over y, z_lo, core), hid: 16 (over x, z_hi).
Axes of the slice: x: 4, y: 4, z: 8 (z_hi: 4, z_lo: 2; z = z_hi * 2 + z_lo), core: 2. Of those that a mesh axis runs over, the one named last changes fastest.
Arguments:
- inputs: bfloat16 [1024, 8192], P('hid', 'row'), may hold values from -6 to 6
- out_grad: bfloat16 [1024, 8192], P('hid', 'row'), may hold values from -2 to 2
- w_in: bfloat16 [8192, 32768], P('row', 'hid'), may hold values from -0.0625 to 0.0625
- w_out: bfloat16 [32768, 8192], P('hid', 'row'), may hold values from -0.03125 to 0.03125
Outputs:
- input_grad: float32 [1024, 8192], P('hid', 'row')
- w_in_grad: float32 [8192, 32768], P('row', 'hid')
- w_out_grad: float32 [32768, 8192], P('hid', 'row')
The draws below stay inside these ranges and needn't reach their ends.
All inputs are finite; a program needn't handle non-finite values.
Results may differ from the reference program's by a relative error of at most 0.0029.
Values may be sent and summed in bfloat16 or wider, within the bound.
A program may use at most 128 MiB of HBM per device.

```python
import jax
import jax.numpy as jnp
from jax import lax

D = 8192
FF = 32768
TOKENS = 1024


def steps_of(own_key, extent, cuts, smallest, high):
    gain = 1.0
    for position, shards_of in cuts:
        draws = jax.random.uniform(jax.random.fold_in(jax.random.fold_in(own_key, 6), position), (shards_of,), jnp.float32, smallest / len(cuts), high / len(cuts))
        gain = gain * jnp.repeat(jnp.exp(draws), extent[position] // shards_of).reshape((-1,) + (1,) * (len(extent) - 1 - position))
    return gain


def centred(stream_key, shape, deviation, reach, split=(), held_as=jnp.bfloat16):
    entries = deviation * jax.random.normal(stream_key, shape, jnp.float32)
    if split:
        entries = entries * steps_of(stream_key, shape, split, -0.22, 0.18)
    return jnp.clip(entries, -reach, reach).astype(held_as)


def setup_inputs(seed: int = 0) -> dict:
    key_list = jax.random.split(jax.random.key(seed), 5)
    inputs = centred(key_list[0], (TOKENS, D), 1.0, 6.0, ((0, 16), (1, 16)))
    out_grad = centred(key_list[1], (TOKENS, D), 0.3, 2.0, ((0, 16), (1, 16)))
    w_in = centred(key_list[2], (D, FF), D ** -0.5, 0.0625, ((0, 16), (1, 16)))
    w_out = centred(key_list[3], (FF, D), FF ** -0.5, 0.03125, ((0, 16), (1, 16)))
    return {"inputs": inputs, "out_grad": out_grad, "w_in": w_in, "w_out": w_out}


def gelu_parts(pre):
    phi = 0.5 * (1.0 + jax.scipy.special.erf(pre * 0.7071067811865476))
    dens = jnp.exp(-0.5 * pre * pre) * 0.3989422804014327
    return pre * phi, phi + pre * dens


def reference(inputs, out_grad, w_in, w_out):
    pre = jnp.dot(inputs, w_in, preferred_element_type=jnp.float32)
    hidden_grad = lax.dot_general(out_grad, w_out, (((1,), (1,)), ((), ())), preferred_element_type=jnp.float32)
    value, slope = gelu_parts(pre)
    act = value.astype(jnp.bfloat16)
    pre_grad = (hidden_grad * slope).astype(jnp.bfloat16)
    w_out_grad = lax.dot_general(act, out_grad, (((0,), (0,)), ((), ())), preferred_element_type=jnp.float32)
    w_in_grad = lax.dot_general(inputs, pre_grad, (((0,), (0,)), ((), ())), preferred_element_type=jnp.float32)
    input_grad = lax.dot_general(pre_grad, w_in, (((1,), (1,)), ((), ())), preferred_element_type=jnp.float32)
    return input_grad, w_in_grad, w_out_grad
```

```python
import functools

import jax
import jax.numpy as jnp
from jax import lax
from jax.experimental import pallas as pl
from jax.experimental.pallas import tpu as pltpu
from jax.sharding import PartitionSpec as P

MESH = pl.DeviceIdType.MESH
F32 = jnp.float32
BF16 = jnp.bfloat16
NC = 4
NT = (((1,), (1,)), ((), ()))

STAGES = {
    "A": (0, 6), "B": (5, 7), "C": (9, 9), "D": (12, 13), "E": (14, 16), "F": (19, 16), "G": (23.5, 16),
    "H": (27.5, 16), "I": (31.5, 16), "J": (38, 16), "K": (42, 16), "L": (45, 16), "M": (48, 16),
    "N": (51, 16), "O": (54, 16),
}
COPIES = [
    "A1", "A2", "A3", "B0", "B1", "C0", "C1", "D",
    "y00", "y01", "y02", "y10", "y11", "y12", "z", "H", "I0", "I1", "J0", "J1", "K",
    "x00", "x01", "x02", "x10", "x11", "x12", "N1", "N2", "N3",
]
NSEM = len(COPIES) * NC + 2


def gelu_parts(pre):
    phi = 0.5 * (1.0 + lax.erf(pre * 0.7071067811865476))
    dens = jnp.exp(-0.5 * pre * pre) * 0.3989422804014327
    return (pre * phi, phi + pre * dens)


UP, DOWN = 2.0**50, 2.0**-50


def encode(v):
    return ((v * UP) * (jnp.abs(v) * UP)).astype(BF16)


def decode(q):
    q = q.astype(F32)
    root = jnp.sqrt(jnp.abs(q)) * DOWN
    return jnp.where(q < 0, -root, root)


def kernel(x_ref, g_ref, w_in, w_out, ig_ref, xo, ao,
           XG, W1, W2, PT, TX, RX, ZT, ZR, ACT, IGP, XR, ZX, ssem, rsem, lsem, wsem):
    r, h = lax.axis_index("row"), lax.axis_index("hid")
    core, zl, y = r % 2, (r // 2) % 2, r // 4
    x, zh = h // 4, h % 4

    def dev(y=y, zl=zl, core=core, x=x, zh=zh):
        return {"row": (y * 2 + zl) * 2 + core, "hid": x * 4 + zh}

    yr, yl, yf = (y + 1) % 4, (y + 3) % 4, (y + 2) % 4
    xr, xl, xf = (x + 1) % 4, (x + 3) % 4, (x + 2) % 4
    right, left = dev(y=yr), dev(y=yl)
    xright, xleft = dev(x=xr), dev(x=xl)
    partner, zpair = dev(core=1 - core), dev(zl=1 - zl)
    zmate = {j: dev(zh=(zh + j) % 4) for j in (1, 2, 3)}

    barrier = pltpu.get_barrier_semaphore()
    others = [right, left, xright, xleft, partner, zpair, zmate[1], zmate[2], zmate[3]]
    for other in others:
        pl.semaphore_signal(barrier, inc=1, device_id=other, device_id_type=MESH)
    pl.semaphore_wait(barrier, len(others))

    copies = {}
    locals_ = []

    def send(name, c, src, dst, to):
        i = COPIES.index(name) + len(COPIES) * c if c is not None else NSEM - 2 + name
        copy = pltpu.make_async_remote_copy(
            src_ref=src, dst_ref=dst, send_sem=ssem.at[i], recv_sem=rsem.at[i], device_id=to, device_id_type=MESH
        )
        copy.start()
        copies[name, c] = copy

    def arrived(c, *names):
        for name in names:
            copies[name, c].wait_recv()

    def keep(src, dst):
        copy = pltpu.make_async_copy(src, dst, lsem.at[len(locals_)])
        copy.start()
        locals_.append(copy)

    def A(c):
        rows = pl.ds(16 * c, 16)
        XG[c, 0, core, h] = x_ref[rows, :]
        XG[c, 1, core, h] = g_ref[rows, :]
        mine = XG.at[c, :, core, h]
        for j in (1, 2, 3):
            send(f"A{j}", c, mine, mine, zmate[j])

    def B(c):
        arrived(c, "A1", "A2", "A3")
        mine = XG.at[c, :, core, pl.ds(4 * x, 4)]
        send("B0", c, mine, mine, xright)
        send("B1", c, mine, mine, xleft)

    def C(c):
        arrived(c, "B0")
        block = XG.at[c, :, core, pl.ds(4 * xl, 2)]
        send("C0", c, block, block, xright)
        arrived(c, "B1")
        block = XG.at[c, :, core, pl.ds(4 * xr + 2, 2)]
        send("C1", c, block, block, xleft)

    def D(c):
        arrived(c, "C0", "C1")
        mine = XG.at[c, :, core]
        send("D", c, mine, mine, partner)
        for a in range(2):
            keep(XG.at[c, a, core], xo.at[a, c])

    def E(c):
        if c == 0:
            copies[0, None].wait_recv()
            copies[1, None].wait_recv()
            for copy in own:
                copy.wait()
        arrived(c, "D")

        @pl.loop(0, 4)
        def _(n):
            cols = pl.ds(pl.multiple_of(n * 256, 256), 256)
            pre = jnp.dot(XG[c, 0, 0].reshape(256, 512), W1[0, :, cols], preferred_element_type=F32)
            pre += jnp.dot(XG[c, 0, 1].reshape(256, 512), W1[1, :, cols], preferred_element_type=F32)
            PT[c, 0, :, :, :, cols] = pre.reshape(4, 2, 32, 256)
            hid = lax.dot_general(XG[c, 1, 0].reshape(256, 512), W2[0, cols, :], NT, preferred_element_type=F32)
            hid += lax.dot_general(XG[c, 1, 1].reshape(256, 512), W2[1, cols, :], NT, preferred_element_type=F32)
            PT[c, 1, :, :, :, cols] = hid.reshape(4, 2, 32, 256)

        for d, kind, piece, half, to in (
            (0, 0, yf, 0, right), (1, 0, yf, 1, left), (0, 1, yr, 1, right), (1, 1, yl, 0, left),
        ):
            for a in range(2):
                TX[c, d, kind, a] = encode(PT[c, a, piece, half])
            send(f"y{d}{kind}", c, TX.at[c, d, kind], RX.at[c, d, kind], to)

    def F(c):
        for d, piece, half, to in ((0, yr, 0, right), (1, yl, 1, left)):
            arrived(c, f"y{d}0")
            for a in range(2):
                TX[c, d, 2, a] = encode(PT[c, a, piece, half] + decode(RX[c, d, 0, a]))
            send(f"y{d}2", c, TX.at[c, d, 2], RX.at[c, d, 2], to)

    def G(c):
        arrived(c, "y01", "y11", "y02", "y12")
        for half in (1 - zl, zl):
            for a in range(2):
                total = PT[c, a, y, half] + decode(RX[c, 0, 2 - half, a]) + decode(RX[c, 1, 1 + half, a])
                if half is zl:
                    PT[c, a, y, half] = total
                else:
                    ZT[c, a] = encode(total)
            if half is not zl:
                send("z", c, ZT.at[c], ZR.at[c], zpair)

    def H(c):
        arrived(c, "z")
        pre = PT[c, 0, y, zl] + decode(ZR[c, 0])
        hidden = PT[c, 1, y, zl] + decode(ZR[c, 1])
        value, slope = gelu_parts(pre)
        ACT[c, 0, core, y, zl] = value.astype(BF16)
        ACT[c, 1, core, y, zl] = (hidden * slope).astype(BF16)
        mine = ACT.at[c, :, core, y, zl]
        send("H", c, mine, mine, zpair)

    def I(c):
        arrived(c, "H")
        mine = ACT.at[c, :, core, y]
        send("I0", c, mine, mine, right)
        send("I1", c, mine, mine, left)

    def J(c):
        arrived(c, "I0")
        block = ACT.at[c, :, core, yl, 0]
        send("J0", c, block, block, right)
        arrived(c, "I1")
        block = ACT.at[c, :, core, yr, 1]
        send("J1", c, block, block, left)

    def K(c):
        arrived(c, "J0", "J1")
        mine = ACT.at[c, :, core]
        send("K", c, mine, mine, partner)

    def L(c):
        arrived(c, "K")
        for a in range(2):
            for k in range(2):
                keep(ACT.at[c, a, k], ao.at[a, c, :, :, :, pl.ds(1024 * k, 1024)])

        @pl.loop(0, 2)
        def _(n):
            rows = pl.ds(pl.multiple_of(n * 256, 256), 256)
            part = lax.dot_general(
                ACT[c, 1, 0].reshape(256, 1024), w_in[rows, :1024], NT, preferred_element_type=F32
            )
            part += lax.dot_general(
                ACT[c, 1, 1].reshape(256, 1024), w_in[rows, 1024:], NT, preferred_element_type=F32
            )
            IGP[c, :, :, :, rows] = part.reshape(4, 2, 32, 256)

        for d, kind, piece, half, to in (
            (0, 0, xf, 0, xright), (1, 0, xf, 1, xleft), (0, 1, xr, 1, xright), (1, 1, xl, 0, xleft),
        ):
            send(f"x{d}{kind}", c, IGP.at[c, piece, half], XR.at[c, d, kind], to)

    def M(c):
        for d, piece, half, to in ((0, xr, 0, xright), (1, xl, 1, xleft)):
            arrived(c, f"x{d}0")
            IGP[c, piece, half] = IGP[c, piece, half] + XR[c, d, 0]
            send(f"x{d}2", c, IGP.at[c, piece, half], XR.at[c, d, 2], to)

    def N(c):
        arrived(c, "x01", "x11", "x02", "x12")
        for half in (0, 1):
            IGP[c, x, half] = IGP[c, x, half] + XR[c, 0, 2 - half] + XR[c, 1, 1 + half]
        for j in (1, 2, 3):
            to = (zh + j) % 4
            send(f"N{j}", c, IGP.at[c, x, to // 2, pl.ds(pl.multiple_of((to % 2) * 16, 16), 16)], ZX.at[c, j - 1], zmate[j])

    def O(c):
        arrived(c, "N1", "N2", "N3")
        own_rows = IGP[c, x, zh // 2, pl.ds(pl.multiple_of((zh % 2) * 16, 16), 16)]
        ig_ref[pl.ds(16 * c, 16), :] = (own_rows + ZX[c, 0]) + (ZX[c, 1] + ZX[c, 2])

    theirs, ours = pl.multiple_of((1 - core) * 1024, 1024), pl.multiple_of(core * 1024, 1024)
    A(0)
    send(0, None, w_in.at[:, pl.ds(theirs, 1024)], W1.at[core], partner)
    send(1, None, w_out.at[pl.ds(theirs, 1024), :], W2.at[core], partner)
    own = [
        pltpu.make_async_copy(w_in.at[:, pl.ds(ours, 1024)], W1.at[core], wsem.at[0]),
        pltpu.make_async_copy(w_out.at[pl.ds(ours, 1024), :], W2.at[core], wsem.at[1]),
    ]
    for copy in own:
        copy.start()

    stages = dict(A=A, B=B, C=C, D=D, E=E, F=F, G=G, H=H, I=I, J=J, K=K, L=L, M=M, N=N, O=O)
    order = sorted((at + step * c, name, c) for name, (at, step) in STAGES.items() for c in range(NC))
    for _, name, c in order:
        if (name, c) != ("A", 0):
            stages[name](c)
    for copy in copies.values():
        copy.wait_send()
    for copy in locals_:
        copy.wait()


def local(inputs, out_grad, w_in, w_out):
    vmem = pl.BlockSpec(memory_space=pltpu.VMEM)
    hbm = pl.BlockSpec(memory_space=pl.ANY)
    input_grad, xg, acts = pl.pallas_call(
        kernel,
        out_shape=(
            jax.ShapeDtypeStruct((64, 512), F32),
            jax.ShapeDtypeStruct((2, NC, 16, 16, 512), BF16),
            jax.ShapeDtypeStruct((2, NC, 4, 2, 32, 2048), BF16),
        ),
        in_specs=[vmem] * 4,
        out_specs=(vmem, hbm, hbm),
        scratch_shapes=[
            pltpu.VMEM((NC, 2, 2, 16, 16, 512), BF16),
            pltpu.VMEM((2, 512, 1024), BF16),
            pltpu.VMEM((2, 1024, 512), BF16),
            pltpu.VMEM((NC, 2, 4, 2, 32, 1024), F32),
            pltpu.VMEM((NC, 2, 3, 2, 32, 1024), BF16),
            pltpu.VMEM((NC, 2, 3, 2, 32, 1024), BF16),
            pltpu.VMEM((NC, 2, 32, 1024), BF16),
            pltpu.VMEM((NC, 2, 32, 1024), BF16),
            pltpu.VMEM((NC, 2, 2, 4, 2, 32, 1024), BF16),
            pltpu.VMEM((NC, 4, 2, 32, 512), F32),
            pltpu.VMEM((NC, 2, 3, 32, 512), F32),
            pltpu.VMEM((NC, 3, 16, 512), F32),
            pltpu.SemaphoreType.DMA((NSEM,)),
            pltpu.SemaphoreType.DMA((NSEM,)),
            pltpu.SemaphoreType.DMA((6 * NC,)),
            pltpu.SemaphoreType.DMA((2,)),
        ],
        compiler_params=pltpu.CompilerParams(
            collective_id=0, has_side_effects=True, vmem_limit_bytes=60 * 2**20
        ),
        cost_estimate=pl.CostEstimate(flops=6 * 2**30, bytes_accessed=16 * 2**20, transcendentals=0),
    )(inputs, out_grad, w_in, w_out)
    xg = xg.reshape(2, 1024, 512)
    acts = acts.reshape(2, 1024, 2048)
    tn = (((0,), (0,)), ((), ()))
    w_out_grad = lax.dot_general(acts[0], xg[1], tn, preferred_element_type=F32)
    w_in_grad = lax.dot_general(xg[0], acts[1], tn, preferred_element_type=F32)
    return (input_grad, w_in_grad, w_out_grad)


def solution(mesh):
    return jax.shard_map(
        local,
        mesh=mesh,
        in_specs=(P("hid", "row"), P("hid", "row"), P("row", "hid"), P("hid", "row")),
        out_specs=(P("hid", "row"), P("row", "hid"), P("hid", "row")),
        check_vma=False,
    )
```

```python
import jax
import jax.numpy as jnp
from jax import lax
from jax.experimental import pallas as pl
from jax.experimental.pallas import tpu as pltpu
from jax.sharding import PartitionSpec as P

MESH = pl.DeviceIdType.MESH
F32 = jnp.float32
BF16 = jnp.bfloat16
NC = 4
Q = 2
COPIES = 208
NT = (((1,), (1,)), ((), ()))

Z_FIRST = ((0, 1), (1, 1), (2, 1), (3, 1),)
Y_FIRST = ((0, 1), (1, 0), (2, 0),)
ORDER = (
    ("A", 0, 0), ("A", 1, 0), ("A", 2, 0), ("A", 3, 0), ("C0", 0, 0), ("B1", 0, 0),
    ("C0", 1, 0), ("B3", 0, 0), ("C0", 2, 0), ("C0", 3, 0), ("B2", 0, 0), ("B1", 1, 0),
    ("C1", 0, 0), ("C3", 0, 0), ("B3", 1, 0), ("C2", 0, 0), ("B2", 1, 0), ("B1", 2, 0),
    ("B3", 2, 0), ("C3", 1, 0), ("C1", 1, 0), ("B2", 2, 0), ("C2", 1, 0), ("D", 0, 0),
    ("B1", 3, 0), ("B3", 3, 0), ("C3", 2, 0), ("C1", 2, 0), ("B2", 3, 0), ("E", 0, 1),
    ("D", 1, 0), ("C2", 2, 0), ("E", 0, 0), ("C3", 3, 0), ("C1", 3, 0), ("E", 1, 0),
    ("D", 2, 0), ("C2", 3, 0), ("E", 1, 1), ("F1", 0, 0), ("F0", 0, 0), ("E", 2, 0),
    ("D", 3, 0), ("F1", 1, 0), ("e", 0, 1), ("E", 2, 1), ("F0", 1, 0), ("E", 3, 1),
    ("E", 3, 0), ("F1", 2, 0), ("F0", 2, 0), ("G", 0, 0), ("e", 1, 1), ("F0", 0, 1),
    ("F1", 0, 1), ("G", 1, 0), ("F1", 3, 0), ("F0", 3, 0), ("e", 2, 1), ("G", 2, 0),
    ("F1", 1, 1), ("F0", 1, 1), ("H", 0, 1), ("G", 3, 0), ("F1", 2, 1), ("F0", 2, 1),
    ("e", 3, 1), ("H", 1, 1), ("H", 0, 0), ("J0", 0, 1), ("J1", 0, 1), ("H", 1, 0),
    ("H", 2, 1), ("F1", 3, 1), ("F0", 3, 1), ("H", 2, 0), ("k", 0, 1), ("H", 3, 0),
    ("J0", 1, 0), ("J1", 1, 0), ("I", 1, 1), ("H", 3, 1), ("I", 0, 0), ("J0", 2, 0),
    ("J1", 2, 0), ("k", 1, 0), ("I", 2, 1), ("J0", 1, 1), ("J1", 1, 1), ("J0", 0, 0),
    ("J1", 0, 0), ("K", 0, 1), ("k", 2, 0), ("I", 3, 0), ("I", 3, 1), ("J0", 2, 1),
    ("J1", 2, 1), ("K", 1, 1), ("K", 0, 0), ("K", 1, 0), ("L", 0, 0), ("J0", 3, 0),
    ("J1", 3, 0), ("L", 0, 1), ("L", 1, 0), ("L", 1, 1), ("J0", 3, 1), ("J1", 3, 1),
    ("M0", 0, 1), ("M1", 0, 1), ("K", 2, 1), ("K", 2, 0), ("M0", 1, 1), ("M1", 1, 1),
    ("K", 3, 0), ("N", 0, 1), ("K", 3, 1), ("L", 2, 0), ("L", 2, 1), ("L", 3, 0),
    ("N", 1, 1), ("L", 3, 1), ("O", 0, 1), ("M0", 2, 1), ("M1", 2, 1), ("O", 1, 1),
    ("M0", 3, 1), ("M1", 3, 1), ("N", 2, 1), ("N", 3, 1), ("O", 2, 1), ("O", 3, 1),
)


def gelu_parts(pre):
    phi = 0.5 * (1.0 + lax.erf(pre * 0.7071067811865476))
    dens = jnp.exp(-0.5 * pre * pre) * 0.3989422804014327
    return (pre * phi, phi + pre * dens)


UP, DOWN = 2.0**50, 2.0**-50
UP_IG, DOWN_IG = 2.0**40, 2.0**-40


def encode(v, up=UP):
    return ((v * up) * (jnp.abs(v) * up)).astype(BF16)


def decode(q, down=DOWN):
    q = q.astype(F32)
    root = jnp.sqrt(jnp.abs(q)) * down
    return jnp.where(q < 0, -root, root)


def kernel(x_ref, g_ref, w_in, w_out, ig_ref, xo, ao,
           XG, WV, W1, W2, PT, TX, RX, ZT, ZR, ACT, IGP, XT, XR, NX, ZX, ssem, rsem, lsem, wsem):
    r, h = lax.axis_index("row"), lax.axis_index("hid")
    core, zl, y = r % 2, (r // 2) % 2, r // 4
    x, zh = h // 4, h % 4

    def dev(y=y, zl=zl, core=core, x=x, zh=zh):
        return {"row": (y * 2 + zl) * 2 + core, "hid": x * 4 + zh}

    yr, yl, yf = (y + 1) % 4, (y + 3) % 4, (y + 2) % 4
    xr, xl, xf = (x + 1) % 4, (x + 3) % 4, (x + 2) % 4
    right, left = dev(y=yr), dev(y=yl)
    xright, xleft = dev(x=xr), dev(x=xl)
    partner, zpair = dev(core=1 - core), dev(zl=1 - zl)
    zmate = {j: dev(zh=(zh + j) % 4) for j in (1, 2, 3)}
    behind = {j: (zh + 4 - j) % 4 for j in (0, 1, 2, 3)}

    barrier = pltpu.get_barrier_semaphore()
    others = [right, left, xright, xleft, partner, zpair, zmate[1], zmate[2], zmate[3]]
    for other in others:
        pl.semaphore_signal(barrier, inc=1, device_id=other, device_id_type=MESH)
    pl.semaphore_wait(barrier, len(others))

    copies = {}
    locals_ = []

    def send(key, src, dst, to):
        i = len(copies)
        copy = pltpu.make_async_remote_copy(
            src_ref=src, dst_ref=dst, send_sem=ssem.at[i], recv_sem=rsem.at[i], device_id=to, device_id_type=MESH
        )
        copy.start()
        copies[key] = copy

    def arrived(*keys):
        for key in keys:
            copies[key].wait_recv()

    def keep(src, dst):
        copy = pltpu.make_async_copy(src, dst, lsem.at[len(locals_)])
        copy.start()
        locals_.append(copy)

    def A(c, u):
        rows = pl.ds(16 * c, 16)
        XG[c, 0, core, h] = x_ref[rows, :]
        XG[c, 1, core, h] = g_ref[rows, :]
        mine = XG.at[c, :, core, h]
        for j in (1, 3, 2):
            send((f"A{j}", c), mine, mine, zmate[j])
        send(("B0r", c), mine, mine, xright)
        send(("B0l", c), mine, mine, xleft)

    def B(j, c):
        arrived((f"A{j}", c))
        block = XG.at[c, :, core, 4 * x + behind[j]]
        send((f"B{j}r", c), block, block, xright)
        send((f"B{j}l", c), block, block, xleft)

    def C(j, c):
        if j < 2:
            arrived((f"B{j}r", c))
            block = XG.at[c, :, core, 4 * xl + behind[j]]
            send((f"C{j}", c), block, block, xright)
        else:
            arrived((f"B{j}l", c))
            block = XG.at[c, :, core, 4 * xr + behind[j]]
            send((f"C{j}", c), block, block, xleft)

    def D(c, u):
        arrived(("C0", c), ("C1", c), ("C2", c), ("C3", c), ("B2r", c), ("B3r", c), ("B0l", c), ("B1l", c))
        mine = XG.at[c, :, core]
        send(("D", c), mine, mine, partner)
        for a in range(2):
            keep(XG.at[c, a, core], xo.at[a, c])

    ready = []

    def E(c, u):
        if not ready:
            arrived("w_in", "w_out")
            for copy in own:
                copy.wait()
        if ("D", c) not in ready:
            arrived(("D", c))
        ready.append(("D", c))

        @pl.loop(0, 2)
        def _(n):
            cols = pl.ds(pl.multiple_of(n * 256, 256), 256)
            wide = pl.ds(pl.multiple_of(n * 256 + 512 * u, 256), 256)
            pre = jnp.dot(XG[c, 0, 0].reshape(256, 512), W1[0, :, wide], preferred_element_type=F32)
            pre += jnp.dot(XG[c, 0, 1].reshape(256, 512), W1[1, :, wide], preferred_element_type=F32)
            PT[c, u, 0, :, :, :, cols] = pre.reshape(4, 2, 32, 256)
            hid = lax.dot_general(XG[c, 1, 0].reshape(256, 512), W2[0, wide, :], NT, preferred_element_type=F32)
            hid += lax.dot_general(XG[c, 1, 1].reshape(256, 512), W2[1, wide, :], NT, preferred_element_type=F32)
            PT[c, u, 1, :, :, :, cols] = hid.reshape(4, 2, 32, 256)

        if (c, u) in Z_FIRST:
            for a in range(2):
                ZT[c, u, a] = encode(PT[c, u, a, :, 1 - zl])
            send(("z", c, u), ZT.at[c, u], ZR.at[c, u], zpair)
        else:
            tree(c, u)

    def e(c, u):
        arrived(("z", c, u))
        for a in range(2):
            PT[c, u, a, :, zl] = PT[c, u, a, :, zl] + decode(ZR[c, u, a])
        tree(c, u)

    def part(c, u, a, piece, half):
        if (c, u) in Z_FIRST:
            return PT.at[c, u, a, piece, zl, pl.ds(16 * half, 16)]
        return PT.at[c, u, a, piece, half]

    def rows_of(c, u):
        return pl.ds(0, 16 if (c, u) in Z_FIRST else 32)

    def tree(c, u):
        rows = rows_of(c, u)
        for d, kind, piece, half, to in (
            (0, 0, yf, 0, right), (1, 0, yf, 1, left), (0, 1, yr, 1, right), (1, 1, yl, 0, left),
        ):
            for a in range(2):
                TX[c, u, d, kind, a, rows] = encode(part(c, u, a, piece, half)[...])
            send((f"y{d}{kind}", c, u), TX.at[c, u, d, kind, :, rows], RX.at[c, u, d, kind, :, rows], to)

    def F(d, c, u):
        rows = rows_of(c, u)
        piece, half, to = ((yr, 0, right), (yl, 1, left))[d]
        arrived((f"y{d}0", c, u))
        for a in range(2):
            TX[c, u, d, 2, a, rows] = encode(part(c, u, a, piece, half)[...] + decode(RX[c, u, d, 0, a, rows]))
        send((f"y{d}2", c, u), TX.at[c, u, d, 2, :, rows], RX.at[c, u, d, 2, :, rows], to)

    def own_sum(c, u, a, half):
        rows = rows_of(c, u)
        return (
            part(c, u, a, y, half)[...]
            + decode(RX[c, u, 0, 2 - half, a, rows])
            + decode(RX[c, u, 1, 1 + half, a, rows])
        )

    def G(c, u):
        arrived(*((f"y{d}{kind}", c, u) for d in range(2) for kind in (1, 2)))
        for a in range(2):
            ZT[c, u, a, 0] = encode(own_sum(c, u, a, 1 - zl))
        send(("z", c, u), ZT.at[c, u, :, 0], ZR.at[c, u, :, 0], zpair)
        for a in range(2):
            PT[c, u, a, y, zl] = own_sum(c, u, a, zl)

    def H(c, u):
        if (c, u) in Z_FIRST:
            arrived(*((f"y{d}{kind}", c, u) for d in range(2) for kind in (1, 2)))
            for half in range(2):
                rows = pl.ds(16 * half, 16)
                value, slope = gelu_parts(own_sum(c, u, 0, half))
                ACT[c, 0, core, u, y, zl, rows] = value.astype(BF16)
                ACT[c, 1, core, u, y, zl, rows] = (own_sum(c, u, 1, half) * slope).astype(BF16)
        else:
            arrived(("z", c, u))
            value, slope = gelu_parts(PT[c, u, 0, y, zl] + decode(ZR[c, u, 0, 0]))
            hidden = PT[c, u, 1, y, zl] + decode(ZR[c, u, 1, 0])
            ACT[c, 0, core, u, y, zl] = value.astype(BF16)
            ACT[c, 1, core, u, y, zl] = (hidden * slope).astype(BF16)
        mine = ACT.at[c, :, core, u, y, zl]
        if (c, u) in Y_FIRST:
            send(("I0", c, u), mine, mine, right)
            send(("I1", c, u), mine, mine, left)
        else:
            send(("H", c, u), mine, mine, zpair)

    def I(c, u):
        arrived(("H", c, u))
        mine = ACT.at[c, :, core, u, y]
        send(("I0", c, u), mine, mine, right)
        send(("I1", c, u), mine, mine, left)

    def J(d, c, u):
        arrived((f"I{d}", c, u))
        piece, to = ((yl, right), (yr, left))[d]
        if (c, u) in Y_FIRST:
            block = ACT.at[c, :, core, u, piece, zl, pl.ds(16 * d, 16)]
        else:
            block = ACT.at[c, :, core, u, piece, d]
        send((f"J{d}", c, u), block, block, to)

    def k(c, u):
        arrived(("J0", c, u), ("J1", c, u))
        mine = ACT.at[c, :, core, u, :, zl]
        send(("k", c, u), mine, mine, zpair)

    def K(c, u):
        arrived(*([("k", c, u)] if (c, u) in Y_FIRST else [("J0", c, u), ("J1", c, u)]))
        mine = ACT.at[c, :, core, u]
        send(("K", c, u), mine, mine, partner)

    def L(c, u):
        arrived(("K", c, u))
        for a in range(2):
            for half in range(2):
                keep(ACT.at[c, a, half, u], ao.at[a, c, :, :, :, pl.ds(1024 * half + 512 * u, 512)])

        @pl.loop(0, 2)
        def _(n):
            rows = pl.ds(pl.multiple_of(n * 256, 256), 256)
            total = jnp.zeros((256, 256), F32)
            for half in range(2):
                total += lax.dot_general(
                    ACT[c, 1, half, u].reshape(256, 512), WV[rows, pl.ds(1024 * half + 512 * u, 512)], NT,
                    preferred_element_type=F32,
                )
            total = total.reshape(4, 2, 32, 256)
            IGP[c, :, :, :, rows] = total if u == 0 else IGP[c, :, :, :, rows] + total

        if u == 0:
            return
        for d, kind, piece, half, to in (
            (0, 0, xf, 0, xright), (1, 0, xf, 1, xleft), (0, 1, xr, 1, xright), (1, 1, xl, 0, xleft),
        ):
            XT[c, d, kind] = encode(IGP[c, piece, half], UP_IG)
            send((f"x{d}{kind}", c), XT.at[c, d, kind], XR.at[c, d, kind], to)

    def M(d, c):
        piece, half, to = ((xr, 0, xright), (xl, 1, xleft))[d]
        arrived((f"x{d}0", c))
        XT[c, d, 2] = encode(IGP[c, piece, half] + decode(XR[c, d, 0], DOWN_IG), UP_IG)
        send((f"x{d}2", c), XT.at[c, d, 2], XR.at[c, d, 2], to)

    def N(c, u):
        arrived(*((f"x{d}{kind}", c) for d in range(2) for kind in (1, 2)))
        for half in (0, 1):
            IGP[c, x, half] = (
                IGP[c, x, half] + decode(XR[c, 0, 2 - half], DOWN_IG) + decode(XR[c, 1, 1 + half], DOWN_IG)
            )
        for j in (1, 2, 3):
            NX[c, j - 1] = encode(rows_for(c, (zh + j) % 4), UP_IG)
            send((f"N{j}", c), NX.at[c, j - 1], ZX.at[c, j - 1], zmate[j])

    def rows_for(c, to):
        return IGP[c, x, to // 2, pl.ds(pl.multiple_of((to % 2) * 16, 16), 16)]

    def O(c, u):
        arrived(("N1", c), ("N2", c), ("N3", c))
        others = decode(ZX[c, 0], DOWN_IG) + decode(ZX[c, 1], DOWN_IG) + decode(ZX[c, 2], DOWN_IG)
        ig_ref[pl.ds(16 * c, 16), :] = rows_for(c, zh) + others

    stages = dict(A=A, D=D, E=E, e=e, G=G, H=H, I=I, k=k, K=K, L=L, N=N, O=O)
    for j in (1, 2, 3):
        stages[f"B{j}"] = lambda c, u, j=j: B(j, c)
    for j in range(4):
        stages[f"C{j}"] = lambda c, u, j=j: C(j, c)
    for d in range(2):
        stages[f"F{d}"] = lambda c, u, d=d: F(d, c, u)
        stages[f"J{d}"] = lambda c, u, d=d: J(d, c, u)
        stages[f"M{d}"] = lambda c, u, d=d: M(d, c)

    theirs, ours = pl.multiple_of((1 - core) * 1024, 1024), pl.multiple_of(core * 1024, 1024)
    own = [
        pltpu.make_async_copy(w_in.at[:, pl.ds(ours, 1024)], W1.at[core], wsem.at[0]),
        pltpu.make_async_copy(w_out.at[pl.ds(ours, 1024), :], W2.at[core], wsem.at[1]),
        pltpu.make_async_copy(w_in, WV, wsem.at[2]),
    ]
    for i, (stage, c, u) in enumerate(ORDER):
        stages[stage](c, u)
        if i == 0:
            send("w_in", w_in.at[:, pl.ds(theirs, 1024)], W1.at[core], partner)
            send("w_out", w_out.at[pl.ds(theirs, 1024), :], W2.at[core], partner)
            for copy in own:
                copy.start()
    for copy in copies.values():
        copy.wait_send()
    for copy in locals_:
        copy.wait()


def local(inputs, out_grad, w_in, w_out):
    vmem = pl.BlockSpec(memory_space=pltpu.VMEM)
    hbm = pl.BlockSpec(memory_space=pl.ANY)
    input_grad, xg, acts = pl.pallas_call(
        kernel,
        out_shape=(
            jax.ShapeDtypeStruct((64, 512), F32),
            jax.ShapeDtypeStruct((2, NC, 16, 16, 512), BF16),
            jax.ShapeDtypeStruct((2, NC, 4, 2, 32, 2048), BF16),
        ),
        in_specs=[vmem, vmem, hbm, hbm],
        out_specs=(vmem, hbm, hbm),
        scratch_shapes=[
            pltpu.VMEM((NC, 2, 2, 16, 16, 512), BF16),
            pltpu.VMEM((512, 2048), BF16),
            pltpu.VMEM((2, 512, 1024), BF16),
            pltpu.VMEM((2, 1024, 512), BF16),
            pltpu.VMEM((NC, Q, 2, 4, 2, 32, 512), F32),
            pltpu.VMEM((NC, Q, 2, 3, 2, 32, 512), BF16),
            pltpu.VMEM((NC, Q, 2, 3, 2, 32, 512), BF16),
            pltpu.VMEM((NC, Q, 2, 4, 32, 512), BF16),
            pltpu.VMEM((NC, Q, 2, 4, 32, 512), BF16),
            pltpu.VMEM((NC, 2, 2, Q, 4, 2, 32, 512), BF16),
            pltpu.VMEM((NC, 4, 2, 32, 512), F32),
            pltpu.VMEM((NC, 2, 3, 32, 512), BF16),
            pltpu.VMEM((NC, 2, 3, 32, 512), BF16),
            pltpu.VMEM((NC, 3, 16, 512), BF16),
            pltpu.VMEM((NC, 3, 16, 512), BF16),
            pltpu.SemaphoreType.DMA((COPIES,)),
            pltpu.SemaphoreType.DMA((COPIES,)),
            pltpu.SemaphoreType.DMA((10 * NC,)),
            pltpu.SemaphoreType.DMA((3,)),
        ],
        compiler_params=pltpu.CompilerParams(
            collective_id=0, has_side_effects=True, vmem_limit_bytes=60 * 2**20
        ),
        cost_estimate=pl.CostEstimate(flops=6 * 2**30, bytes_accessed=16 * 2**20, transcendentals=0),
    )(inputs, out_grad, w_in, w_out)
    xg = xg.reshape(2, 1024, 512)
    acts = acts.reshape(2, 1024, 2048)
    tn = (((0,), (0,)), ((), ()))
    w_out_grad = lax.dot_general(acts[0], xg[1], tn, preferred_element_type=F32)
    w_in_grad = lax.dot_general(xg[0], acts[1], tn, preferred_element_type=F32)
    return (input_grad, w_in_grad, w_out_grad)


def solution(mesh):
    return jax.shard_map(
        local,
        mesh=mesh,
        in_specs=(P("hid", "row"), P("hid", "row"), P("row", "hid"), P("hid", "row")),
        out_specs=(P("hid", "row"), P("row", "hid"), P("hid", "row")),
        check_vma=False,
    )
```

```python
import jax
import jax.numpy as jnp
from jax import lax
from jax.experimental import pallas as pl
from jax.experimental.pallas import tpu as pltpu
from jax.sharding import PartitionSpec as P

MESH = pl.DeviceIdType.MESH
F32 = jnp.float32
BF16 = jnp.bfloat16
NC = 4
Q = 2
COPIES = 208
NT = (((1,), (1,)), ((), ()))
TN = (((0,), (0,)), ((), ()))

Z_FIRST = ((1, 1), (2, 0), (3, 0),)
Y_FIRST = ((0, 0), (1, 1), (2, 1),)
ORDER = (
    ("A", 0, 0), ("A", 1, 0), ("B1", 0, 0), ("B3", 0, 0), ("B2", 0, 0), ("B1", 1, 0),
    ("B3", 1, 0), ("B2", 1, 0), ("A", 2, 0), ("D", 0, 0), ("B1", 2, 0), ("E", 0, 0),
    ("B3", 2, 0), ("D", 1, 0), ("B2", 2, 0), ("A", 3, 0), ("E", 0, 1), ("F0", 0, 0),
    ("E", 1, 1), ("B1", 3, 0), ("F1", 0, 0), ("B3", 3, 0), ("D", 2, 0), ("B2", 3, 0),
    ("F1", 0, 1), ("F0", 0, 1), ("E", 1, 0), ("E", 2, 1), ("G", 0, 0), ("E", 2, 0),
    ("D", 3, 0), ("e", 1, 1), ("G", 0, 1), ("F1", 1, 0), ("F0", 1, 0), ("H", 0, 0),
    ("E", 3, 1), ("E", 3, 0), ("F1", 2, 1), ("F0", 2, 1), ("F0", 1, 1), ("F1", 1, 1),
    ("G", 1, 0), ("e", 2, 0), ("J0", 0, 0), ("J1", 0, 0), ("H", 0, 1), ("F0", 3, 1),
    ("F1", 3, 1), ("G", 2, 1), ("H", 1, 1), ("F0", 2, 0), ("F1", 2, 0), ("e", 3, 0),
    ("k", 0, 0), ("H", 1, 0), ("G", 3, 1), ("I", 0, 1), ("J0", 1, 1), ("J1", 1, 1),
    ("H", 2, 1), ("H", 2, 0), ("F0", 3, 0), ("F1", 3, 0), ("J0", 0, 1), ("J1", 0, 1),
    ("k", 1, 1), ("K", 0, 0), ("J0", 2, 1), ("J1", 2, 1), ("I", 1, 0), ("H", 3, 0),
    ("L", 0, 0), ("H", 3, 1), ("K", 0, 1), ("k", 2, 1), ("I", 2, 0), ("L", 0, 1),
    ("J0", 1, 0), ("J1", 1, 0), ("J0", 2, 0), ("J1", 2, 0), ("K", 1, 1), ("K", 1, 0),
    ("I", 3, 0), ("N", 0, 1), ("I", 3, 1), ("K", 2, 0), ("L", 1, 0), ("L", 1, 1),
    ("L", 2, 0), ("J0", 3, 0), ("J1", 3, 0), ("K", 2, 1), ("J0", 3, 1), ("J1", 3, 1),
    ("O", 0, 1), ("N", 1, 1), ("K", 3, 0), ("L", 2, 1), ("K", 3, 1), ("L", 3, 0),
    ("O", 1, 1), ("L", 3, 1), ("N", 2, 1), ("O", 2, 1), ("N", 3, 1), ("O", 3, 1),
)


def gelu_parts(pre):
    phi = 0.5 * (1.0 + lax.erf(pre * 0.7071067811865476))
    dens = jnp.exp(-0.5 * pre * pre) * 0.3989422804014327
    return (pre * phi, phi + pre * dens)


UP, DOWN = 2.0**50, 2.0**-50
UP_IG, DOWN_IG = 2.0**40, 2.0**-40


def encode(v, up=UP):
    return ((v * up) * (jnp.abs(v) * up)).astype(BF16)


def decode(q, down=DOWN):
    q = q.astype(F32)
    root = jnp.sqrt(jnp.abs(q)) * down
    return jnp.where(q < 0, -root, root)


def kernel(x_ref, g_ref, w_in, w_out, ig_ref, xo, go, ao, po,
           XG, WV, W1, W2, PT, TX, RX, ZT, ZR, ACT, IGP, XT, XR, NX, ZX, ssem, rsem, lsem, wsem):
    r, h = lax.axis_index("row"), lax.axis_index("hid")
    core, zl, y = r % 2, (r // 2) % 2, r // 4
    x, zh = h // 4, h % 4

    def dev(y=y, zl=zl, core=core, x=x, zh=zh):
        return {"row": (y * 2 + zl) * 2 + core, "hid": x * 4 + zh}

    yr, yl, yf = (y + 1) % 4, (y + 3) % 4, (y + 2) % 4
    right, left = dev(y=yr), dev(y=yl)
    partner, zpair = dev(core=1 - core), dev(zl=1 - zl)
    xmate = {j: dev(x=(x + j) % 4) for j in (1, 2, 3)}
    zmate = {j: dev(zh=(zh + j) % 4) for j in (1, 2, 3)}
    behind = {j: (zh + 4 - j) % 4 for j in (0, 1, 2, 3)}

    barrier = pltpu.get_barrier_semaphore()
    others = [right, left, partner, zpair, *xmate.values(), *zmate.values()]
    for other in others:
        pl.semaphore_signal(barrier, inc=1, device_id=other, device_id_type=MESH)
    pl.semaphore_wait(barrier, len(others))

    copies = {}
    locals_ = []

    def send(key, src, dst, to):
        i = len(copies)
        copy = pltpu.make_async_remote_copy(
            src_ref=src, dst_ref=dst, send_sem=ssem.at[i], recv_sem=rsem.at[i], device_id=to, device_id_type=MESH
        )
        copy.start()
        copies[key] = copy

    def arrived(*keys):
        for key in keys:
            copies[key].wait_recv()

    def keep(src, dst):
        copy = pltpu.make_async_copy(src, dst, lsem.at[len(locals_)])
        copy.start()
        locals_.append(copy)

    def A(c, u):
        rows = pl.ds(16 * c, 16)
        XG[c, 0, core, h] = x_ref[rows, :]
        XG[c, 1, core, h] = g_ref[rows, :]
        mine = XG.at[c, :, core, h]
        for j in (1, 3, 2):
            send((f"A{j}", c), mine, mine, zmate[j])
        across(0, c)

    def across(j, c):
        block = XG.at[c, :, core, 4 * x + behind[j]]
        for i in (1, 3, 2):
            send((f"B{j}{i}", c), block, block, xmate[i])

    def B(j, c):
        arrived((f"A{j}", c))
        across(j, c)

    def D(c, u):
        arrived(*((f"B{j}{i}", c) for j in range(4) for i in (1, 2, 3)))
        mine = XG.at[c, :, core]
        send(("D", c), mine, mine, partner)
        keep(XG.at[c, 0, core], xo.at[c])
        keep(XG.at[c, 1, core], go.at[c])

    ready = []

    def E(c, u):
        if not ready:
            arrived("w_in", "w_out")
            for copy in own:
                copy.wait()
        if ("D", c) not in ready:
            arrived(("D", c))
        ready.append(("D", c))

        @pl.loop(0, 2)
        def _(n):
            cols = pl.ds(pl.multiple_of(n * 256, 256), 256)
            wide = pl.ds(pl.multiple_of(n * 256 + 512 * u, 256), 256)
            pre = jnp.dot(XG[c, 0, 0].reshape(256, 512), W1[0, :, wide], preferred_element_type=F32)
            pre += jnp.dot(XG[c, 0, 1].reshape(256, 512), W1[1, :, wide], preferred_element_type=F32)
            PT[c, u, 0, :, :, :, cols] = pre.reshape(4, 2, 32, 256)
            hid = lax.dot_general(XG[c, 1, 0].reshape(256, 512), W2[0, wide, :], NT, preferred_element_type=F32)
            hid += lax.dot_general(XG[c, 1, 1].reshape(256, 512), W2[1, wide, :], NT, preferred_element_type=F32)
            PT[c, u, 1, :, :, :, cols] = hid.reshape(4, 2, 32, 256)

        if (c, u) in Z_FIRST:
            for a in range(2):
                ZT[c, u, a] = encode(PT[c, u, a, :, 1 - zl])
            send(("z", c, u), ZT.at[c, u], ZR.at[c, u], zpair)
        else:
            tree(c, u)

    def e(c, u):
        arrived(("z", c, u))
        for a in range(2):
            PT[c, u, a, :, zl] = PT[c, u, a, :, zl] + decode(ZR[c, u, a])
        tree(c, u)

    def part(c, u, a, piece, half):
        if (c, u) in Z_FIRST:
            return PT.at[c, u, a, piece, zl, pl.ds(16 * half, 16)]
        return PT.at[c, u, a, piece, half]

    def rows_of(c, u):
        return pl.ds(0, 16 if (c, u) in Z_FIRST else 32)

    def tree(c, u):
        rows = rows_of(c, u)
        for d, kind, piece, half, to in (
            (0, 0, yf, 0, right), (1, 0, yf, 1, left), (0, 1, yr, 1, right), (1, 1, yl, 0, left),
        ):
            for a in range(2):
                TX[c, u, d, kind, a, rows] = encode(part(c, u, a, piece, half)[...])
            send((f"y{d}{kind}", c, u), TX.at[c, u, d, kind, :, rows], RX.at[c, u, d, kind, :, rows], to)

    def F(d, c, u):
        rows = rows_of(c, u)
        piece, half, to = ((yr, 0, right), (yl, 1, left))[d]
        arrived((f"y{d}0", c, u))
        for a in range(2):
            TX[c, u, d, 2, a, rows] = encode(part(c, u, a, piece, half)[...] + decode(RX[c, u, d, 0, a, rows]))
        send((f"y{d}2", c, u), TX.at[c, u, d, 2, :, rows], RX.at[c, u, d, 2, :, rows], to)

    def own_sum(c, u, a, half):
        rows = rows_of(c, u)
        return (
            part(c, u, a, y, half)[...]
            + decode(RX[c, u, 0, 2 - half, a, rows])
            + decode(RX[c, u, 1, 1 + half, a, rows])
        )

    def G(c, u):
        arrived(*((f"y{d}{kind}", c, u) for d in range(2) for kind in (1, 2)))
        for a in range(2):
            ZT[c, u, a, 0] = encode(own_sum(c, u, a, 1 - zl))
        send(("z", c, u), ZT.at[c, u, :, 0], ZR.at[c, u, :, 0], zpair)
        for a in range(2):
            PT[c, u, a, y, zl] = own_sum(c, u, a, zl)

    def H(c, u):
        if (c, u) in Z_FIRST:
            arrived(*((f"y{d}{kind}", c, u) for d in range(2) for kind in (1, 2)))
            for half in range(2):
                rows = pl.ds(16 * half, 16)
                value, slope = gelu_parts(own_sum(c, u, 0, half))
                ACT[c, 0, core, u, y, zl, rows] = value.astype(BF16)
                ACT[c, 1, core, u, y, zl, rows] = (own_sum(c, u, 1, half) * slope).astype(BF16)
        else:
            arrived(("z", c, u))
            value, slope = gelu_parts(PT[c, u, 0, y, zl] + decode(ZR[c, u, 0, 0]))
            hidden = PT[c, u, 1, y, zl] + decode(ZR[c, u, 1, 0])
            ACT[c, 0, core, u, y, zl] = value.astype(BF16)
            ACT[c, 1, core, u, y, zl] = (hidden * slope).astype(BF16)
        mine = ACT.at[c, :, core, u, y, zl]
        if (c, u) in Y_FIRST:
            send(("I0", c, u), mine, mine, right)
            send(("I1", c, u), mine, mine, left)
        else:
            send(("H", c, u), mine, mine, zpair)

    def I(c, u):
        arrived(("H", c, u))
        mine = ACT.at[c, :, core, u, y]
        send(("I0", c, u), mine, mine, right)
        send(("I1", c, u), mine, mine, left)

    def J(d, c, u):
        arrived((f"I{d}", c, u))
        piece, to = ((yl, right), (yr, left))[d]
        if (c, u) in Y_FIRST:
            block = ACT.at[c, :, core, u, piece, zl, pl.ds(16 * d, 16)]
        else:
            block = ACT.at[c, :, core, u, piece, d]
        send((f"J{d}", c, u), block, block, to)

    def k(c, u):
        arrived(("J0", c, u), ("J1", c, u))
        mine = ACT.at[c, :, core, u, :, zl]
        send(("k", c, u), mine, mine, zpair)

    def K(c, u):
        arrived(*([("k", c, u)] if (c, u) in Y_FIRST else [("J0", c, u), ("J1", c, u)]))
        mine = ACT.at[c, :, core, u]
        send(("K", c, u), mine, mine, partner)

    def L(c, u):
        arrived(("K", c, u))
        for a in range(2):
            for half in range(2):
                keep(ACT.at[c, a, half, u], (ao, po)[a].at[c, :, :, :, pl.ds(1024 * half + 512 * u, 512)])

        @pl.loop(0, 2)
        def _(n):
            rows = pl.ds(pl.multiple_of(n * 256, 256), 256)
            total = jnp.zeros((256, 256), F32)
            for half in range(2):
                total += lax.dot_general(
                    ACT[c, 1, half, u].reshape(256, 512), WV[rows, pl.ds(1024 * half + 512 * u, 512)], NT,
                    preferred_element_type=F32,
                )
            total = total.reshape(4, 2, 32, 256)
            IGP[c, :, :, :, rows] = total if u == 0 else IGP[c, :, :, :, rows] + total

        if u == 0:
            return
        for j in (1, 3, 2):
            XT[c, j - 1] = encode(IGP[c, (x + j) % 4], UP_IG)
            send((f"x{j}", c), XT.at[c, j - 1], XR.at[c, j - 1], xmate[j])

    def N(c, u):
        arrived(("x1", c), ("x2", c), ("x3", c))
        others = decode(XR[c, 0], DOWN_IG) + decode(XR[c, 1], DOWN_IG) + decode(XR[c, 2], DOWN_IG)
        IGP[c, x] = IGP[c, x] + others
        for j in (1, 2, 3):
            NX[c, j - 1] = encode(rows_for(c, (zh + j) % 4), UP_IG)
            send((f"N{j}", c), NX.at[c, j - 1], ZX.at[c, j - 1], zmate[j])

    def rows_for(c, to):
        return IGP[c, x, to // 2, pl.ds(pl.multiple_of((to % 2) * 16, 16), 16)]

    def O(c, u):
        arrived(("N1", c), ("N2", c), ("N3", c))
        others = decode(ZX[c, 0], DOWN_IG) + decode(ZX[c, 1], DOWN_IG) + decode(ZX[c, 2], DOWN_IG)
        ig_ref[pl.ds(16 * c, 16), :] = rows_for(c, zh) + others

    stages = dict(A=A, D=D, E=E, e=e, G=G, H=H, I=I, k=k, K=K, L=L, N=N, O=O)
    for j in (1, 2, 3):
        stages[f"B{j}"] = lambda c, u, j=j: B(j, c)
    for d in range(2):
        stages[f"F{d}"] = lambda c, u, d=d: F(d, c, u)
        stages[f"J{d}"] = lambda c, u, d=d: J(d, c, u)

    theirs, ours = pl.multiple_of((1 - core) * 1024, 1024), pl.multiple_of(core * 1024, 1024)
    own = [
        pltpu.make_async_copy(w_in.at[:, pl.ds(ours, 1024)], W1.at[core], wsem.at[0]),
        pltpu.make_async_copy(w_out.at[pl.ds(ours, 1024), :], W2.at[core], wsem.at[1]),
        pltpu.make_async_copy(w_in, WV, wsem.at[2]),
    ]
    for i, (stage, c, u) in enumerate(ORDER):
        stages[stage](c, u)
        if i == 0:
            send("w_in", w_in.at[:, pl.ds(theirs, 1024)], W1.at[core], partner)
            send("w_out", w_out.at[pl.ds(theirs, 1024), :], W2.at[core], partner)
            for copy in own:
                copy.start()
    for copy in copies.values():
        copy.wait_send()
    for copy in locals_:
        copy.wait()


def local(inputs, out_grad, w_in, w_out):
    vmem = pl.BlockSpec(memory_space=pltpu.VMEM)
    hbm = pl.BlockSpec(memory_space=pl.ANY)
    input_grad, xg, gg, act, pre_grad = pl.pallas_call(
        kernel,
        out_shape=(
            jax.ShapeDtypeStruct((64, 512), F32),
            jax.ShapeDtypeStruct((NC, 16, 16, 512), BF16),
            jax.ShapeDtypeStruct((NC, 16, 16, 512), BF16),
            jax.ShapeDtypeStruct((NC, 4, 2, 32, 2048), BF16),
            jax.ShapeDtypeStruct((NC, 4, 2, 32, 2048), BF16),
        ),
        in_specs=[vmem, vmem, hbm, hbm],
        out_specs=(vmem, hbm, hbm, hbm, hbm),
        scratch_shapes=[
            pltpu.VMEM((NC, 2, 2, 16, 16, 512), BF16),
            pltpu.VMEM((512, 2048), BF16),
            pltpu.VMEM((2, 512, 1024), BF16),
            pltpu.VMEM((2, 1024, 512), BF16),
            pltpu.VMEM((NC, Q, 2, 4, 2, 32, 512), F32),
            pltpu.VMEM((NC, Q, 2, 3, 2, 32, 512), BF16),
            pltpu.VMEM((NC, Q, 2, 3, 2, 32, 512), BF16),
            pltpu.VMEM((NC, Q, 2, 4, 32, 512), BF16),
            pltpu.VMEM((NC, Q, 2, 4, 32, 512), BF16),
            pltpu.VMEM((NC, 2, 2, Q, 4, 2, 32, 512), BF16),
            pltpu.VMEM((NC, 4, 2, 32, 512), F32),
            pltpu.VMEM((NC, 3, 2, 32, 512), BF16),
            pltpu.VMEM((NC, 3, 2, 32, 512), BF16),
            pltpu.VMEM((NC, 3, 16, 512), BF16),
            pltpu.VMEM((NC, 3, 16, 512), BF16),
            pltpu.SemaphoreType.DMA((COPIES,)),
            pltpu.SemaphoreType.DMA((COPIES,)),
            pltpu.SemaphoreType.DMA((10 * NC,)),
            pltpu.SemaphoreType.DMA((3,)),
        ],
        compiler_params=pltpu.CompilerParams(
            collective_id=0, has_side_effects=True, vmem_limit_bytes=60 * 2**20
        ),
        cost_estimate=pl.CostEstimate(flops=6 * 2**30, bytes_accessed=16 * 2**20, transcendentals=0),
    )(inputs, out_grad, w_in, w_out)
    w_in_grad, w_out_grad = weight_grads(
        xg.reshape(1024, 512), gg.reshape(1024, 512), act.reshape(1024, 2048), pre_grad.reshape(1024, 2048)
    )
    return (input_grad, w_in_grad, w_out_grad)


def weight_grads(xg, gg, act, pre_grad):
    steps = 2
    width = 2048 // steps
    whole, columns = pl.BlockSpec((1024, 512), lambda i: (0, 0)), pl.BlockSpec((1024, width), lambda i: (0, i))

    def body(x, g, a, p, w_in_grad, w_out_grad):
        w_in_grad[...] = lax.dot_general(x[...], p[...], TN, preferred_element_type=F32)
        w_out_grad[...] = lax.dot_general(a[...], g[...], TN, preferred_element_type=F32)

    return pl.pallas_call(
        body,
        grid=(steps,),
        out_shape=(jax.ShapeDtypeStruct((512, 2048), F32), jax.ShapeDtypeStruct((2048, 512), F32)),
        in_specs=[whole, whole, columns, columns],
        out_specs=(pl.BlockSpec((512, width), lambda i: (0, i)), pl.BlockSpec((width, 512), lambda i: (i, 0))),
        compiler_params=pltpu.CompilerParams(vmem_limit_bytes=60 * 2**20),
        cost_estimate=pl.CostEstimate(flops=4 * 2**30, bytes_accessed=18 * 2**20, transcendentals=0),
    )(xg, gg, act, pre_grad)


def solution(mesh):
    return jax.shard_map(
        local,
        mesh=mesh,
        in_specs=(P("hid", "row"), P("hid", "row"), P("row", "hid"), P("hid", "row")),
        out_specs=(P("hid", "row"), P("row", "hid"), P("hid", "row")),
        check_vma=False,
    )
```

```python
import jax
import jax.numpy as jnp
from jax import lax
from jax.experimental import pallas as pl
from jax.experimental.pallas import tpu as pltpu
from jax.sharding import PartitionSpec as P

MESH = pl.DeviceIdType.MESH
F32 = jnp.float32
BF16 = jnp.bfloat16
NC = 4
Q = 2
COPIES = 270
NT = (((1,), (1,)), ((), ()))
TN = (((0,), (0,)), ((), ()))

Z_FIRST = ((1, 0), (2, 1), (3, 0),)
Y_FIRST = ((0, 1), (1, 0), (3, 1),)
ORDER = (
    ("Ax", 0, 0), ("A", 1, 0), ("A", 3, 0), ("B1x", 0, 0), ("B3x", 0, 0), ("B2x", 0, 0),
    ("B2", 1, 0), ("B1", 1, 0), ("B3", 1, 0), ("Dx", 0, 0), ("Ag", 0, 0), ("B1", 3, 0),
    ("B2", 3, 0), ("Ex", 0, 1), ("Ex", 0, 0), ("B3", 3, 0), ("A", 2, 0), ("D", 1, 0),
    ("F0x", 0, 1), ("F1x", 0, 1), ("B1g", 0, 0), ("E", 1, 1), ("E", 1, 0), ("F0x", 0, 0),
    ("B3g", 0, 0), ("B2g", 0, 0), ("B2", 2, 0), ("D", 3, 0), ("B3", 2, 0), ("F1x", 0, 0),
    ("F1", 1, 1), ("F0", 1, 1), ("E", 3, 1), ("B1", 2, 0), ("Dg", 0, 0), ("E", 3, 0),
    ("Eg", 0, 0), ("Eg", 0, 1), ("e", 1, 0), ("D", 2, 0), ("F0", 3, 1), ("F1g", 0, 0),
    ("F1", 3, 1), ("E", 2, 1), ("F1g", 0, 1), ("F0g", 0, 0), ("G", 1, 1), ("F0g", 0, 1),
    ("F0", 1, 0), ("F1", 1, 0), ("E", 2, 0), ("e", 3, 0), ("H", 1, 0), ("G", 0, 0),
    ("Sp", 1, 0), ("Sa", 1, 0), ("G", 3, 1), ("e", 2, 1), ("F0", 2, 0), ("G", 0, 1),
    ("F1", 2, 0), ("H", 1, 1), ("H", 0, 0), ("Sp", 1, 1), ("J0p", 1, 0), ("J1p", 1, 0),
    ("Sa", 0, 0), ("Sp", 0, 0), ("F1", 3, 0), ("Sa", 1, 1), ("F0", 2, 1), ("H", 3, 1),
    ("Sp", 3, 1), ("F1", 2, 1), ("Sa", 3, 1), ("F0", 3, 0), ("G", 2, 0), ("H", 0, 1),
    ("Ip", 1, 1), ("Sp", 0, 1), ("kp", 1, 0), ("Ip", 0, 0), ("H", 3, 0), ("J0a", 3, 1),
    ("H", 2, 0), ("J1a", 1, 0), ("Sp", 3, 0), ("Sp", 2, 0), ("J0p", 3, 1), ("J0a", 1, 0),
    ("J1p", 1, 1), ("H", 2, 1), ("J0p", 0, 1), ("J1p", 0, 1), ("Sp", 2, 1), ("J1p", 3, 1),
    ("Sa", 3, 0), ("J0p", 1, 1), ("Sa", 2, 0), ("J1a", 3, 1), ("J0p", 0, 0), ("J1p", 0, 0),
    ("Ip", 3, 0), ("kp", 0, 1), ("Ip", 2, 0), ("Ip", 2, 1), ("Sa", 0, 1), ("kp", 3, 1),
    ("Kp", 1, 0), ("Kp", 1, 1), ("L", 1, 0), ("Kp", 0, 0), ("L", 1, 1), ("Sa", 2, 1),
    ("J1p", 3, 0), ("J0p", 2, 0), ("J1p", 2, 0), ("J0p", 3, 0), ("Kp", 0, 1), ("J0p", 2, 1),
    ("J1p", 2, 1), ("ka", 3, 1), ("L", 0, 0), ("L", 0, 1), ("J1a", 0, 1), ("Ia", 3, 0),
    ("J0a", 0, 1), ("ka", 1, 0), ("Kp", 2, 0), ("Ia", 0, 0), ("Ia", 2, 0), ("Kp", 3, 0),
    ("Kp", 2, 1), ("Kp", 3, 1), ("Ia", 2, 1), ("L", 2, 0), ("L", 2, 1), ("N", 1, 1),
    ("Ia", 1, 1), ("L", 3, 0), ("ka", 0, 1), ("N", 0, 1), ("J1a", 3, 0), ("J0a", 3, 0),
    ("L", 3, 1), ("J0a", 2, 0), ("N", 2, 1), ("J0a", 2, 1), ("Ka", 1, 0), ("J0a", 0, 0),
    ("J1a", 2, 0), ("J0a", 1, 1), ("J1a", 0, 0), ("J1a", 1, 1), ("J1a", 2, 1), ("Ka", 3, 1),
    ("N", 3, 1), ("Q", 1, 0), ("Ka", 3, 0), ("Ka", 2, 0), ("Ka", 0, 1), ("Q", 3, 1),
    ("Ka", 1, 1), ("O", 1, 1), ("Ka", 0, 0), ("Q", 3, 0), ("Ka", 2, 1), ("O", 2, 1),
    ("Q", 2, 0), ("O", 0, 1), ("Q", 0, 0), ("Q", 1, 1), ("Q", 0, 1), ("Q", 2, 1),
    ("O", 3, 1),
)


def gelu_parts(pre):
    phi = 0.5 * (1.0 + lax.erf(pre * 0.7071067811865476))
    dens = jnp.exp(-0.5 * pre * pre) * 0.3989422804014327
    return (pre * phi, phi + pre * dens)


UP, DOWN = 2.0**50, 2.0**-50
UP_IG, DOWN_IG = 2.0**40, 2.0**-40


def encode(v, up=UP):
    return ((v * up) * (jnp.abs(v) * up)).astype(BF16)


def decode(q, down=DOWN):
    q = q.astype(F32)
    root = jnp.sqrt(jnp.abs(q)) * down
    return jnp.where(q < 0, -root, root)


def kernel(x_ref, g_ref, w_in, w_out, ig_ref, xo, go, ao, po,
           XG, WV, W1, W2, PT, TX, RX, ZT, ZR, ACT, IGP, XT, XR, NX, ZX, ssem, rsem, lsem, wsem):
    r, h = lax.axis_index("row"), lax.axis_index("hid")
    core, zl, y = r % 2, (r // 2) % 2, r // 4
    x, zh = h // 4, h % 4

    def dev(y=y, zl=zl, core=core, x=x, zh=zh):
        return {"row": (y * 2 + zl) * 2 + core, "hid": x * 4 + zh}

    yr, yl, yf = (y + 1) % 4, (y + 3) % 4, (y + 2) % 4
    right, left = dev(y=yr), dev(y=yl)
    partner, zpair = dev(core=1 - core), dev(zl=1 - zl)
    xmate = {j: dev(x=(x + j) % 4) for j in (1, 2, 3)}
    zmate = {j: dev(zh=(zh + j) % 4) for j in (1, 2, 3)}
    behind = {j: (zh + 4 - j) % 4 for j in (0, 1, 2, 3)}

    barrier = pltpu.get_barrier_semaphore()
    others = [right, left, partner, zpair, *xmate.values(), *zmate.values()]
    for other in others:
        pl.semaphore_signal(barrier, inc=1, device_id=other, device_id_type=MESH)
    pl.semaphore_wait(barrier, len(others))

    copies = {}
    locals_ = []

    def send(key, src, dst, to):
        i = len(copies)
        copy = pltpu.make_async_remote_copy(
            src_ref=src, dst_ref=dst, send_sem=ssem.at[i], recv_sem=rsem.at[i], device_id=to, device_id_type=MESH
        )
        copy.start()
        copies[key] = copy

    def arrived(*keys):
        for key in keys:
            copies[key].wait_recv()

    def keep(src, dst):
        copy = pltpu.make_async_copy(src, dst, lsem.at[len(locals_)])
        copy.start()
        locals_.append(copy)

    arrays = {"": (0, 1), "x": (0,), "g": (1,)}
    span = {"": slice(None), "x": pl.ds(0, 1), "g": pl.ds(1, 1)}

    def versions(c):
        return ("x", "g") if c == 0 else ("",)

    def A(c, u, v):
        rows = pl.ds(16 * c, 16)
        for a in arrays[v]:
            XG[c, a, core, h] = (x_ref, g_ref)[a][rows, :]
        mine = XG.at[c, span[v], core, h]
        for j in (2, 1, 3):
            send((f"A{j}{v}", c), mine, mine, zmate[j])
        across(0, c, v)

    def across(j, c, v):
        block = XG.at[c, span[v], core, 4 * x + behind[j]]
        for i in (2, 1, 3):
            send((f"B{j}{i}{v}", c), block, block, xmate[i])

    def B(j, c, v):
        arrived((f"A{j}{v}", c))
        across(j, c, v)

    def D(c, u, v):
        arrived(*((f"B{j}{i}{v}", c) for j in range(4) for i in (1, 2, 3)))
        mine = XG.at[c, span[v], core]
        send((f"D{v}", c), mine, mine, partner)
        for a in arrays[v]:
            keep(XG.at[c, a, core], (xo, go)[a].at[c])

    ready = []

    def once(key, wait):
        if key not in ready:
            wait()
        ready.append(key)

    def E(c, u, v):
        for a in arrays[v]:
            once(("w", a), lambda a=a: (arrived(("w_in", "w_out")[a]), own[a].wait()))
        once(("D", c, v), lambda: arrived((f"D{v}", c)))

        @pl.loop(0, 2)
        def _(n):
            cols = pl.ds(pl.multiple_of(n * 256, 256), 256)
            wide = pl.ds(pl.multiple_of(n * 256 + 512 * u, 256), 256)
            if 0 in arrays[v]:
                pre = jnp.dot(XG[c, 0, 0].reshape(256, 512), W1[0, :, wide], preferred_element_type=F32)
                pre += jnp.dot(XG[c, 0, 1].reshape(256, 512), W1[1, :, wide], preferred_element_type=F32)
                PT[c, u, 0, :, :, :, cols] = pre.reshape(4, 2, 32, 256)
            if 1 in arrays[v]:
                hid = lax.dot_general(XG[c, 1, 0].reshape(256, 512), W2[0, wide, :], NT, preferred_element_type=F32)
                hid += lax.dot_general(XG[c, 1, 1].reshape(256, 512), W2[1, wide, :], NT, preferred_element_type=F32)
                PT[c, u, 1, :, :, :, cols] = hid.reshape(4, 2, 32, 256)

        if (c, u) in Z_FIRST:
            for a in range(2):
                ZT[c, u, a] = encode(PT[c, u, a, :, 1 - zl])
            send(("z", c, u), ZT.at[c, u], ZR.at[c, u], zpair)
        else:
            tree(c, u, v)

    def e(c, u):
        arrived(("z", c, u))
        for a in range(2):
            PT[c, u, a, :, zl] = PT[c, u, a, :, zl] + decode(ZR[c, u, a])
        tree(c, u, "")

    def part(c, u, a, piece, half):
        if (c, u) in Z_FIRST:
            return PT.at[c, u, a, piece, zl, pl.ds(16 * half, 16)]
        return PT.at[c, u, a, piece, half]

    def rows_of(c, u):
        return pl.ds(0, 16 if (c, u) in Z_FIRST else 32)

    def tree(c, u, v):
        rows = rows_of(c, u)
        for d, kind, piece, half, to in (
            (0, 0, yf, 0, right), (1, 0, yf, 1, left), (0, 1, yr, 1, right), (1, 1, yl, 0, left),
        ):
            for a in arrays[v]:
                TX[c, u, d, kind, a, rows] = encode(part(c, u, a, piece, half)[...])
            send((f"y{d}{kind}{v}", c, u), TX.at[c, u, d, kind, span[v], rows], RX.at[c, u, d, kind, span[v], rows], to)

    def F(d, c, u, v):
        rows = rows_of(c, u)
        piece, half, to = ((yr, 0, right), (yl, 1, left))[d]
        arrived((f"y{d}0{v}", c, u))
        for a in arrays[v]:
            TX[c, u, d, 2, a, rows] = encode(part(c, u, a, piece, half)[...] + decode(RX[c, u, d, 0, a, rows]))
        send((f"y{d}2{v}", c, u), TX.at[c, u, d, 2, span[v], rows], RX.at[c, u, d, 2, span[v], rows], to)

    def sums(c, u):
        arrived(*((f"y{d}{kind}{v}", c, u) for d in range(2) for kind in (1, 2) for v in versions(c)))

    def own_sum(c, u, a, half):
        rows = rows_of(c, u)
        return (
            part(c, u, a, y, half)[...]
            + decode(RX[c, u, 0, 2 - half, a, rows])
            + decode(RX[c, u, 1, 1 + half, a, rows])
        )

    def G(c, u):
        sums(c, u)
        for a in range(2):
            ZT[c, u, a, 0] = encode(own_sum(c, u, a, 1 - zl))
        send(("z", c, u), ZT.at[c, u, :, 0], ZR.at[c, u, :, 0], zpair)
        for a in range(2):
            PT[c, u, a, y, zl] = own_sum(c, u, a, zl)

    def H(c, u):
        if (c, u) in Z_FIRST:
            sums(c, u)
            for half in range(2):
                rows = pl.ds(16 * half, 16)
                value, slope = gelu_parts(own_sum(c, u, 0, half))
                ACT[c, 0, core, u, y, zl, rows] = value.astype(BF16)
                ACT[c, 1, core, u, y, zl, rows] = (own_sum(c, u, 1, half) * slope).astype(BF16)
        else:
            arrived(("z", c, u))
            value, slope = gelu_parts(PT[c, u, 0, y, zl] + decode(ZR[c, u, 0, 0]))
            hidden = PT[c, u, 1, y, zl] + decode(ZR[c, u, 1, 0])
            ACT[c, 0, core, u, y, zl] = value.astype(BF16)
            ACT[c, 1, core, u, y, zl] = (hidden * slope).astype(BF16)

    def S(a, c, u):
        mine = ACT.at[c, a, core, u, y, zl]
        if (c, u) in Y_FIRST:
            send(("I0", a, c, u), mine, mine, right)
            send(("I1", a, c, u), mine, mine, left)
        else:
            send(("S", a, c, u), mine, mine, zpair)

    def I(a, c, u):
        arrived(("S", a, c, u))
        mine = ACT.at[c, a, core, u, y]
        send(("I0", a, c, u), mine, mine, right)
        send(("I1", a, c, u), mine, mine, left)

    def J(d, a, c, u):
        arrived((f"I{d}", a, c, u))
        piece, to = ((yl, right), (yr, left))[d]
        if (c, u) in Y_FIRST:
            block = ACT.at[c, a, core, u, piece, zl, pl.ds(16 * d, 16)]
        else:
            block = ACT.at[c, a, core, u, piece, d]
        send((f"J{d}", a, c, u), block, block, to)

    def k(a, c, u):
        arrived(("J0", a, c, u), ("J1", a, c, u))
        mine = ACT.at[c, a, core, u, :, zl]
        send(("k", a, c, u), mine, mine, zpair)

    def K(a, c, u):
        arrived(*([("k", a, c, u)] if (c, u) in Y_FIRST else [("J0", a, c, u), ("J1", a, c, u)]))
        mine = ACT.at[c, a, core, u]
        send(("K", a, c, u), mine, mine, partner)

    def whole(a, c, u):
        arrived(("K", a, c, u))
        for half in range(2):
            keep(ACT.at[c, a, half, u], (ao, po)[a].at[c, :, :, :, pl.ds(1024 * half + 512 * u, 512)])

    def L(c, u):
        whole(1, c, u)
        once(("w", 2), own[2].wait)

        @pl.loop(0, 2)
        def _(n):
            rows = pl.ds(pl.multiple_of(n * 256, 256), 256)
            total = jnp.zeros((256, 256), F32)
            for half in range(2):
                total += lax.dot_general(
                    ACT[c, 1, half, u].reshape(256, 512), WV[rows, pl.ds(1024 * half + 512 * u, 512)], NT,
                    preferred_element_type=F32,
                )
            total = total.reshape(4, 2, 32, 256)
            IGP[c, :, :, :, rows] = total if u == 0 else IGP[c, :, :, :, rows] + total

        if u == 0:
            return
        for j in (2, 1, 3):
            XT[c, j - 1] = encode(IGP[c, (x + j) % 4], UP_IG)
            send((f"x{j}", c), XT.at[c, j - 1], XR.at[c, j - 1], xmate[j])

    def N(c, u):
        arrived(("x1", c), ("x2", c), ("x3", c))
        others = decode(XR[c, 0], DOWN_IG) + decode(XR[c, 1], DOWN_IG) + decode(XR[c, 2], DOWN_IG)
        IGP[c, x] = IGP[c, x] + others
        for j in (2, 1, 3):
            NX[c, j - 1] = encode(rows_for(c, (zh + j) % 4), UP_IG)
            send((f"N{j}", c), NX.at[c, j - 1], ZX.at[c, j - 1], zmate[j])

    def rows_for(c, to):
        return IGP[c, x, to // 2, pl.ds(pl.multiple_of((to % 2) * 16, 16), 16)]

    def O(c, u):
        arrived(("N1", c), ("N2", c), ("N3", c))
        others = decode(ZX[c, 0], DOWN_IG) + decode(ZX[c, 1], DOWN_IG) + decode(ZX[c, 2], DOWN_IG)
        ig_ref[pl.ds(16 * c, 16), :] = rows_for(c, zh) + others

    stages = dict(e=e, G=G, H=H, L=L, N=N, O=O, Q=lambda c, u: whole(0, c, u))
    for v in ("", "x", "g"):
        for name, f in (("A", A), ("D", D), ("E", E)):
            stages[name + v] = lambda c, u, f=f, v=v: f(c, u, v)
        for j in (1, 2, 3):
            stages[f"B{j}{v}"] = lambda c, u, j=j, v=v: B(j, c, v)
        for d in range(2):
            stages[f"F{d}{v}"] = lambda c, u, d=d, v=v: F(d, c, u, v)
    for a, v in enumerate("ap"):
        for name, f in (("S", S), ("I", I), ("k", k), ("K", K)):
            stages[name + v] = lambda c, u, a=a, f=f: f(a, c, u)
        for d in range(2):
            stages[f"J{d}{v}"] = lambda c, u, d=d, a=a: J(d, a, c, u)

    theirs, ours = pl.multiple_of((1 - core) * 1024, 1024), pl.multiple_of(core * 1024, 1024)
    own = [
        pltpu.make_async_copy(w_in.at[:, pl.ds(ours, 1024)], W1.at[core], wsem.at[0]),
        pltpu.make_async_copy(w_out.at[pl.ds(ours, 1024), :], W2.at[core], wsem.at[1]),
        pltpu.make_async_copy(w_in, WV, wsem.at[2]),
    ]
    for i, (stage, c, u) in enumerate(ORDER):
        stages[stage](c, u)
        if i == 0:
            send("w_in", w_in.at[:, pl.ds(theirs, 1024)], W1.at[core], partner)
            send("w_out", w_out.at[pl.ds(theirs, 1024), :], W2.at[core], partner)
            for copy in own:
                copy.start()
    for copy in copies.values():
        copy.wait_send()
    for copy in locals_:
        copy.wait()


def local(inputs, out_grad, w_in, w_out):
    vmem = pl.BlockSpec(memory_space=pltpu.VMEM)
    hbm = pl.BlockSpec(memory_space=pl.ANY)
    input_grad, xg, gg, act, pre_grad = pl.pallas_call(
        kernel,
        out_shape=(
            jax.ShapeDtypeStruct((64, 512), F32),
            jax.ShapeDtypeStruct((NC, 16, 16, 512), BF16),
            jax.ShapeDtypeStruct((NC, 16, 16, 512), BF16),
            jax.ShapeDtypeStruct((NC, 4, 2, 32, 2048), BF16),
            jax.ShapeDtypeStruct((NC, 4, 2, 32, 2048), BF16),
        ),
        in_specs=[vmem, vmem, hbm, hbm],
        out_specs=(vmem, hbm, hbm, hbm, hbm),
        scratch_shapes=[
            pltpu.VMEM((NC, 2, 2, 16, 16, 512), BF16),
            pltpu.VMEM((512, 2048), BF16),
            pltpu.VMEM((2, 512, 1024), BF16),
            pltpu.VMEM((2, 1024, 512), BF16),
            pltpu.VMEM((NC, Q, 2, 4, 2, 32, 512), F32),
            pltpu.VMEM((NC, Q, 2, 3, 2, 32, 512), BF16),
            pltpu.VMEM((NC, Q, 2, 3, 2, 32, 512), BF16),
            pltpu.VMEM((NC, Q, 2, 4, 32, 512), BF16),
            pltpu.VMEM((NC, Q, 2, 4, 32, 512), BF16),
            pltpu.VMEM((NC, 2, 2, Q, 4, 2, 32, 512), BF16),
            pltpu.VMEM((NC, 4, 2, 32, 512), F32),
            pltpu.VMEM((NC, 3, 2, 32, 512), BF16),
            pltpu.VMEM((NC, 3, 2, 32, 512), BF16),
            pltpu.VMEM((NC, 3, 16, 512), BF16),
            pltpu.VMEM((NC, 3, 16, 512), BF16),
            pltpu.SemaphoreType.DMA((COPIES,)),
            pltpu.SemaphoreType.DMA((COPIES,)),
            pltpu.SemaphoreType.DMA((10 * NC,)),
            pltpu.SemaphoreType.DMA((3,)),
        ],
        compiler_params=pltpu.CompilerParams(
            collective_id=0, has_side_effects=True, vmem_limit_bytes=60 * 2**20
        ),
        cost_estimate=pl.CostEstimate(flops=6 * 2**30, bytes_accessed=16 * 2**20, transcendentals=0),
    )(inputs, out_grad, w_in, w_out)
    w_in_grad, w_out_grad = weight_grads(
        xg.reshape(1024, 512), gg.reshape(1024, 512), act.reshape(1024, 2048), pre_grad.reshape(1024, 2048)
    )
    return (input_grad, w_in_grad, w_out_grad)


def weight_grads(xg, gg, act, pre_grad):
    steps = 2
    width = 2048 // steps
    whole, columns = pl.BlockSpec((1024, 512), lambda i: (0, 0)), pl.BlockSpec((1024, width), lambda i: (0, i))

    def body(x, g, a, p, w_in_grad, w_out_grad):
        w_in_grad[...] = lax.dot_general(x[...], p[...], TN, preferred_element_type=F32)
        w_out_grad[...] = lax.dot_general(a[...], g[...], TN, preferred_element_type=F32)

    return pl.pallas_call(
        body,
        grid=(steps,),
        out_shape=(jax.ShapeDtypeStruct((512, 2048), F32), jax.ShapeDtypeStruct((2048, 512), F32)),
        in_specs=[whole, whole, columns, columns],
        out_specs=(pl.BlockSpec((512, width), lambda i: (0, i)), pl.BlockSpec((width, 512), lambda i: (i, 0))),
        compiler_params=pltpu.CompilerParams(vmem_limit_bytes=60 * 2**20),
        cost_estimate=pl.CostEstimate(flops=4 * 2**30, bytes_accessed=18 * 2**20, transcendentals=0),
    )(xg, gg, act, pre_grad)


def solution(mesh):
    return jax.shard_map(
        local,
        mesh=mesh,
        in_specs=(P("hid", "row"), P("hid", "row"), P("row", "hid"), P("hid", "row")),
        out_specs=(P("hid", "row"), P("row", "hid"), P("hid", "row")),
        check_vma=False,
    )
```

```python
import jax
import jax.numpy as jnp
from jax import lax
from jax.experimental import pallas as pl
from jax.experimental.pallas import tpu as pltpu
from jax.sharding import PartitionSpec as P

MESH = pl.DeviceIdType.MESH
F32 = jnp.float32
BF16 = jnp.bfloat16
NC = 4
Q = 2
COPIES = 270
NT = (((1,), (1,)), ((), ()))
TN = (((0,), (0,)), ((), ()))

Z_FIRST = ((1, 0), (3, 1),)
Y_FIRST = ((0, 0), (1, 0), (1, 1),)
ORDER = (
    ("Ax", 0, 0), ("Ag", 0, 0), ("A", 1, 0), ("A", 2, 0), ("B1x", 0, 0), ("B2x", 0, 0),
    ("B3x", 0, 0), ("B2g", 0, 0), ("B3g", 0, 0), ("B1g", 0, 0), ("B2", 1, 0), ("B3", 1, 0),
    ("B1", 1, 0), ("Dx", 0, 0), ("A", 3, 0), ("Ex", 0, 1), ("Dg", 0, 0), ("Ex", 0, 0),
    ("B2", 2, 0), ("B3", 2, 0), ("Eg", 0, 0), ("Eg", 0, 1), ("D", 1, 0), ("F0x", 0, 1),
    ("B1", 2, 0), ("F0x", 0, 0), ("B1", 3, 0), ("F1x", 0, 1), ("B2", 3, 0), ("F1x", 0, 0),
    ("E", 1, 1), ("B3", 3, 0), ("F1g", 0, 0), ("E", 1, 0), ("F1g", 0, 1), ("D", 2, 0),
    ("F0g", 0, 0), ("F0g", 0, 1), ("F0", 1, 1), ("F1", 1, 1), ("E", 2, 1), ("D", 3, 0),
    ("G", 0, 0), ("E", 2, 0), ("G", 0, 1), ("E", 3, 1), ("F1", 2, 1), ("F0", 2, 1),
    ("e", 1, 0), ("H", 0, 0), ("F1", 2, 0), ("Sp", 0, 0), ("F0", 2, 0), ("G", 1, 1),
    ("E", 3, 0), ("F0", 1, 0), ("G", 2, 1), ("F1", 1, 0), ("e", 3, 1), ("G", 2, 0),
    ("H", 0, 1), ("Sp", 0, 1), ("F0", 3, 0), ("F1", 3, 0), ("J1p", 0, 0), ("H", 1, 1),
    ("J0p", 0, 0), ("Sa", 0, 1), ("Sp", 1, 1), ("H", 2, 1), ("H", 1, 0), ("Sp", 1, 0),
    ("Sp", 2, 1), ("H", 2, 0), ("Sp", 2, 0), ("F0", 3, 1), ("Sa", 1, 1), ("Sa", 2, 1),
    ("F1", 3, 1), ("Ip", 0, 1), ("G", 3, 0), ("kp", 0, 0), ("J1p", 1, 0), ("J0p", 1, 0),
    ("J1p", 1, 1), ("Ip", 2, 1), ("H", 3, 1), ("J0p", 1, 1), ("Sp", 3, 1), ("Sa", 1, 0),
    ("H", 3, 0), ("Sp", 3, 0), ("J0p", 0, 1), ("Ip", 2, 0), ("J0a", 1, 1), ("J1a", 1, 1),
    ("kp", 1, 0), ("J1p", 0, 1), ("kp", 1, 1), ("Kp", 0, 0), ("Sa", 0, 0), ("J0p", 2, 1),
    ("J1a", 1, 0), ("J0a", 1, 0), ("Sa", 3, 1), ("Sa", 3, 0), ("Sa", 2, 0), ("Ip", 3, 0),
    ("Ip", 3, 1), ("ka", 1, 1), ("J1p", 2, 0), ("Kp", 0, 1), ("J0p", 2, 0), ("L", 0, 0),
    ("J1p", 2, 1), ("Kp", 1, 0), ("J0a", 0, 0), ("Ia", 0, 1), ("L", 0, 1), ("J1p", 3, 0),
    ("J1a", 0, 0), ("J0p", 3, 0), ("Kp", 1, 1), ("L", 1, 0), ("J1p", 3, 1), ("J0p", 3, 1),
    ("Kp", 2, 1), ("Kp", 2, 0), ("L", 1, 1), ("Ia", 3, 0), ("Ia", 2, 0), ("ka", 1, 0),
    ("L", 2, 0), ("Kp", 3, 0), ("L", 2, 1), ("Kp", 3, 1), ("ka", 0, 0), ("Ia", 2, 1),
    ("L", 3, 0), ("Ia", 3, 1), ("L", 3, 1), ("N", 1, 1), ("N", 0, 1), ("Ka", 1, 1),
    ("J0a", 0, 1), ("J1a", 3, 0), ("J1a", 2, 1), ("J1a", 2, 0), ("J0a", 2, 0), ("J0a", 2, 1),
    ("N", 2, 1), ("Ka", 0, 0), ("J0a", 3, 1), ("J1a", 0, 1), ("J0a", 3, 0), ("J1a", 3, 1),
    ("N", 3, 1), ("Ka", 1, 0), ("Ka", 2, 0), ("Ka", 2, 1), ("O", 0, 1), ("Ka", 0, 1),
    ("Ka", 3, 0), ("Q", 1, 0), ("Ka", 3, 1), ("Q", 2, 1), ("O", 2, 1), ("Q", 0, 0),
    ("Q", 1, 1), ("Q", 0, 1), ("O", 1, 1), ("Q", 2, 0), ("Q", 3, 0), ("Q", 3, 1),
    ("O", 3, 1),
)


def gelu_parts(pre):
    phi = 0.5 * (1.0 + lax.erf(pre * 0.7071067811865476))
    dens = jnp.exp(-0.5 * pre * pre) * 0.3989422804014327
    return (pre * phi, phi + pre * dens)


UP, DOWN = 2.0**50, 2.0**-50
UP_IG, DOWN_IG = 2.0**40, 2.0**-40


def encode(v, up=UP):
    return ((v * up) * (jnp.abs(v) * up)).astype(BF16)


def decode(q, down=DOWN):
    q = q.astype(F32)
    root = jnp.sqrt(jnp.abs(q)) * down
    return jnp.where(q < 0, -root, root)


def kernel(x_ref, g_ref, w_in, w_out, ig_ref, xo, go, ao, po,
           XG, WV, W1, W2, PT, TX, RX, ZT, ZR, ACT, IGP, XT, XR, NX, ZX, ssem, rsem, lsem, wsem):
    r, h = lax.axis_index("row"), lax.axis_index("hid")
    core, zl, y = r % 2, (r // 2) % 2, r // 4
    x, zh = h // 4, h % 4

    def dev(y=y, zl=zl, core=core, x=x, zh=zh):
        return {"row": (y * 2 + zl) * 2 + core, "hid": x * 4 + zh}

    yr, yl, yf = (y + 1) % 4, (y + 3) % 4, (y + 2) % 4
    right, left = dev(y=yr), dev(y=yl)
    partner, zpair = dev(core=1 - core), dev(zl=1 - zl)
    xmate = {j: dev(x=(x + j) % 4) for j in (1, 2, 3)}
    zmate = {j: dev(zh=(zh + j) % 4) for j in (1, 2, 3)}
    behind = {j: (zh + 4 - j) % 4 for j in (0, 1, 2, 3)}

    theirs, ours = pl.multiple_of((1 - core) * 1024, 1024), pl.multiple_of(core * 1024, 1024)
    mine_in = {}
    for c in range(NC):
        for a in range(2):
            mine_in[c, a] = pltpu.make_async_copy(
                (x_ref, g_ref)[a].at[pl.ds(16 * c, 16), :], XG.at[c, a, core, h], wsem.at[3 + 2 * c + a]
            )
            mine_in[c, a].start()
    own = [
        pltpu.make_async_copy(w_in.at[:, pl.ds(ours, 1024)], W1.at[core], wsem.at[0]),
        pltpu.make_async_copy(w_out.at[pl.ds(ours, 1024), :], W2.at[core], wsem.at[1]),
        pltpu.make_async_copy(w_in, WV, wsem.at[2]),
    ]
    for copy in own:
        copy.start()

    barrier = pltpu.get_barrier_semaphore()
    others = [right, left, partner, zpair, *xmate.values(), *zmate.values()]
    for other in others:
        pl.semaphore_signal(barrier, inc=1, device_id=other, device_id_type=MESH)
    pl.semaphore_wait(barrier, len(others))

    copies = {}
    locals_ = []

    def send(key, src, dst, to):
        i = len(copies)
        copy = pltpu.make_async_remote_copy(
            src_ref=src, dst_ref=dst, send_sem=ssem.at[i], recv_sem=rsem.at[i], device_id=to, device_id_type=MESH
        )
        copy.start()
        copies[key] = copy

    def arrived(*keys):
        for key in keys:
            copies[key].wait_recv()

    def keep(src, dst):
        copy = pltpu.make_async_copy(src, dst, lsem.at[len(locals_)])
        copy.start()
        locals_.append(copy)

    arrays = {"": (0, 1), "x": (0,), "g": (1,)}
    span = {"": slice(None), "x": pl.ds(0, 1), "g": pl.ds(1, 1)}

    def versions(c):
        return ("x", "g") if c == 0 else ("",)

    def A(c, u, v):
        for a in arrays[v]:
            mine_in[c, a].wait()
        mine = XG.at[c, span[v], core, h]
        for j in (2, 1, 3):
            send((f"A{j}{v}", c), mine, mine, zmate[j])
        across(0, c, v)

    def across(j, c, v):
        block = XG.at[c, span[v], core, 4 * x + behind[j]]
        for i in (2, 1, 3):
            send((f"B{j}{i}{v}", c), block, block, xmate[i])

    def B(j, c, v):
        arrived((f"A{j}{v}", c))
        across(j, c, v)

    def D(c, u, v):
        arrived(*((f"B{j}{i}{v}", c) for j in range(4) for i in (1, 2, 3)))
        mine = XG.at[c, span[v], core]
        send((f"D{v}", c), mine, mine, partner)
        for a in arrays[v]:
            keep(XG.at[c, a, core], (xo, go)[a].at[c])

    ready = []

    def once(key, wait):
        if key not in ready:
            wait()
        ready.append(key)

    def E(c, u, v):
        for a in arrays[v]:
            once(("w", a), lambda a=a: (arrived(("w_in", "w_out")[a]), own[a].wait()))
        once(("D", c, v), lambda: arrived((f"D{v}", c)))

        @pl.loop(0, 2)
        def _(n):
            cols = pl.ds(pl.multiple_of(n * 256, 256), 256)
            wide = pl.ds(pl.multiple_of(n * 256 + 512 * u, 256), 256)
            if 0 in arrays[v]:
                pre = jnp.dot(XG[c, 0, 0].reshape(256, 512), W1[0, :, wide], preferred_element_type=F32)
                pre += jnp.dot(XG[c, 0, 1].reshape(256, 512), W1[1, :, wide], preferred_element_type=F32)
                PT[c, u, 0, :, :, :, cols] = pre.reshape(4, 2, 32, 256)
            if 1 in arrays[v]:
                hid = lax.dot_general(XG[c, 1, 0].reshape(256, 512), W2[0, wide, :], NT, preferred_element_type=F32)
                hid += lax.dot_general(XG[c, 1, 1].reshape(256, 512), W2[1, wide, :], NT, preferred_element_type=F32)
                PT[c, u, 1, :, :, :, cols] = hid.reshape(4, 2, 32, 256)

        if (c, u) in Z_FIRST:
            for a in range(2):
                ZT[c, u, a] = encode(PT[c, u, a, :, 1 - zl])
            send(("z", c, u), ZT.at[c, u], ZR.at[c, u], zpair)
        else:
            tree(c, u, v)

    def e(c, u):
        arrived(("z", c, u))
        for a in range(2):
            PT[c, u, a, :, zl] = PT[c, u, a, :, zl] + decode(ZR[c, u, a])
        tree(c, u, "")

    def part(c, u, a, piece, half):
        if (c, u) in Z_FIRST:
            return PT.at[c, u, a, piece, zl, pl.ds(16 * half, 16)]
        return PT.at[c, u, a, piece, half]

    def rows_of(c, u):
        return pl.ds(0, 16 if (c, u) in Z_FIRST else 32)

    def tree(c, u, v):
        rows = rows_of(c, u)
        for d, kind, piece, half, to in (
            (0, 0, yf, 0, right), (1, 0, yf, 1, left), (0, 1, yr, 1, right), (1, 1, yl, 0, left),
        ):
            for a in arrays[v]:
                TX[c, u, d, kind, a, rows] = encode(part(c, u, a, piece, half)[...])
            send((f"y{d}{kind}{v}", c, u), TX.at[c, u, d, kind, span[v], rows], RX.at[c, u, d, kind, span[v], rows], to)

    def F(d, c, u, v):
        rows = rows_of(c, u)
        piece, half, to = ((yr, 0, right), (yl, 1, left))[d]
        arrived((f"y{d}0{v}", c, u))
        for a in arrays[v]:
            TX[c, u, d, 2, a, rows] = encode(part(c, u, a, piece, half)[...] + decode(RX[c, u, d, 0, a, rows]))
        send((f"y{d}2{v}", c, u), TX.at[c, u, d, 2, span[v], rows], RX.at[c, u, d, 2, span[v], rows], to)

    def sums(c, u):
        arrived(*((f"y{d}{kind}{v}", c, u) for d in range(2) for kind in (1, 2) for v in versions(c)))

    def own_sum(c, u, a, half):
        rows = rows_of(c, u)
        return (
            part(c, u, a, y, half)[...]
            + decode(RX[c, u, 0, 2 - half, a, rows])
            + decode(RX[c, u, 1, 1 + half, a, rows])
        )

    def G(c, u):
        sums(c, u)
        for a in range(2):
            ZT[c, u, a, 0] = encode(own_sum(c, u, a, 1 - zl))
        send(("z", c, u), ZT.at[c, u, :, 0], ZR.at[c, u, :, 0], zpair)
        for a in range(2):
            PT[c, u, a, y, zl] = own_sum(c, u, a, zl)

    def H(c, u):
        if (c, u) in Z_FIRST:
            sums(c, u)
            for half in range(2):
                rows = pl.ds(16 * half, 16)
                value, slope = gelu_parts(own_sum(c, u, 0, half))
                ACT[c, 0, core, u, y, zl, rows] = value.astype(BF16)
                ACT[c, 1, core, u, y, zl, rows] = (own_sum(c, u, 1, half) * slope).astype(BF16)
        else:
            arrived(("z", c, u))
            value, slope = gelu_parts(PT[c, u, 0, y, zl] + decode(ZR[c, u, 0, 0]))
            hidden = PT[c, u, 1, y, zl] + decode(ZR[c, u, 1, 0])
            ACT[c, 0, core, u, y, zl] = value.astype(BF16)
            ACT[c, 1, core, u, y, zl] = (hidden * slope).astype(BF16)

    def S(a, c, u):
        mine = ACT.at[c, a, core, u, y, zl]
        if (c, u) in Y_FIRST:
            send(("I0", a, c, u), mine, mine, right)
            send(("I1", a, c, u), mine, mine, left)
        else:
            send(("S", a, c, u), mine, mine, zpair)

    def I(a, c, u):
        arrived(("S", a, c, u))
        mine = ACT.at[c, a, core, u, y]
        send(("I0", a, c, u), mine, mine, right)
        send(("I1", a, c, u), mine, mine, left)

    def J(d, a, c, u):
        arrived((f"I{d}", a, c, u))
        piece, to = ((yl, right), (yr, left))[d]
        if (c, u) in Y_FIRST:
            block = ACT.at[c, a, core, u, piece, zl, pl.ds(16 * d, 16)]
        else:
            block = ACT.at[c, a, core, u, piece, d]
        send((f"J{d}", a, c, u), block, block, to)

    def k(a, c, u):
        arrived(("J0", a, c, u), ("J1", a, c, u))
        mine = ACT.at[c, a, core, u, :, zl]
        send(("k", a, c, u), mine, mine, zpair)

    def K(a, c, u):
        arrived(*([("k", a, c, u)] if (c, u) in Y_FIRST else [("J0", a, c, u), ("J1", a, c, u)]))
        mine = ACT.at[c, a, core, u]
        send(("K", a, c, u), mine, mine, partner)

    def whole(a, c, u):
        arrived(("K", a, c, u))
        for half in range(2):
            keep(ACT.at[c, a, half, u], (ao, po)[a].at[c, :, :, :, pl.ds(1024 * half + 512 * u, 512)])

    def L(c, u):
        whole(1, c, u)
        once(("w", 2), own[2].wait)

        @pl.loop(0, 2)
        def _(n):
            rows = pl.ds(pl.multiple_of(n * 256, 256), 256)
            total = jnp.zeros((256, 256), F32)
            for half in range(2):
                total += lax.dot_general(
                    ACT[c, 1, half, u].reshape(256, 512), WV[rows, pl.ds(1024 * half + 512 * u, 512)], NT,
                    preferred_element_type=F32,
                )
            total = total.reshape(4, 2, 32, 256)
            IGP[c, :, :, :, rows] = total if u == 0 else IGP[c, :, :, :, rows] + total

        if u == 0:
            return
        for j in (2, 1, 3):
            XT[c, j - 1] = encode(IGP[c, (x + j) % 4], UP_IG)
            send((f"x{j}", c), XT.at[c, j - 1], XR.at[c, j - 1], xmate[j])

    def N(c, u):
        arrived(("x1", c), ("x2", c), ("x3", c))
        others = decode(XR[c, 0], DOWN_IG) + decode(XR[c, 1], DOWN_IG) + decode(XR[c, 2], DOWN_IG)
        IGP[c, x] = IGP[c, x] + others
        for j in (2, 1, 3):
            NX[c, j - 1] = encode(rows_for(c, (zh + j) % 4), UP_IG)
            send((f"N{j}", c), NX.at[c, j - 1], ZX.at[c, j - 1], zmate[j])

    def rows_for(c, to):
        return IGP[c, x, to // 2, pl.ds(pl.multiple_of((to % 2) * 16, 16), 16)]

    def O(c, u):
        arrived(("N1", c), ("N2", c), ("N3", c))
        others = decode(ZX[c, 0], DOWN_IG) + decode(ZX[c, 1], DOWN_IG) + decode(ZX[c, 2], DOWN_IG)
        ig_ref[pl.ds(16 * c, 16), :] = rows_for(c, zh) + others

    stages = dict(e=e, G=G, H=H, L=L, N=N, O=O, Q=lambda c, u: whole(0, c, u))
    for v in ("", "x", "g"):
        for name, f in (("A", A), ("D", D), ("E", E)):
            stages[name + v] = lambda c, u, f=f, v=v: f(c, u, v)
        for j in (1, 2, 3):
            stages[f"B{j}{v}"] = lambda c, u, j=j, v=v: B(j, c, v)
        for d in range(2):
            stages[f"F{d}{v}"] = lambda c, u, d=d, v=v: F(d, c, u, v)
    for a, v in enumerate("ap"):
        for name, f in (("S", S), ("I", I), ("k", k), ("K", K)):
            stages[name + v] = lambda c, u, a=a, f=f: f(a, c, u)
        for d in range(2):
            stages[f"J{d}{v}"] = lambda c, u, d=d, a=a: J(d, a, c, u)

    for i, (stage, c, u) in enumerate(ORDER):
        stages[stage](c, u)
        if i == 0:
            send("w_in", w_in.at[:, pl.ds(theirs, 1024)], W1.at[core], partner)
            send("w_out", w_out.at[pl.ds(theirs, 1024), :], W2.at[core], partner)
    for copy in copies.values():
        copy.wait_send()
    for copy in locals_:
        copy.wait()


def local(inputs, out_grad, w_in, w_out):
    vmem = pl.BlockSpec(memory_space=pltpu.VMEM)
    hbm = pl.BlockSpec(memory_space=pl.ANY)
    input_grad, xg, gg, act, pre_grad = pl.pallas_call(
        kernel,
        out_shape=(
            jax.ShapeDtypeStruct((64, 512), F32),
            jax.ShapeDtypeStruct((NC, 16, 16, 512), BF16),
            jax.ShapeDtypeStruct((NC, 16, 16, 512), BF16),
            jax.ShapeDtypeStruct((NC, 4, 2, 32, 2048), BF16),
            jax.ShapeDtypeStruct((NC, 4, 2, 32, 2048), BF16),
        ),
        in_specs=[hbm] * 4,
        out_specs=(vmem, hbm, hbm, hbm, hbm),
        scratch_shapes=[
            pltpu.VMEM((NC, 2, 2, 16, 16, 512), BF16),
            pltpu.VMEM((512, 2048), BF16),
            pltpu.VMEM((2, 512, 1024), BF16),
            pltpu.VMEM((2, 1024, 512), BF16),
            pltpu.VMEM((NC, Q, 2, 4, 2, 32, 512), F32),
            pltpu.VMEM((NC, Q, 2, 3, 2, 32, 512), BF16),
            pltpu.VMEM((NC, Q, 2, 3, 2, 32, 512), BF16),
            pltpu.VMEM((NC, Q, 2, 4, 32, 512), BF16),
            pltpu.VMEM((NC, Q, 2, 4, 32, 512), BF16),
            pltpu.VMEM((NC, 2, 2, Q, 4, 2, 32, 512), BF16),
            pltpu.VMEM((NC, 4, 2, 32, 512), F32),
            pltpu.VMEM((NC, 3, 2, 32, 512), BF16),
            pltpu.VMEM((NC, 3, 2, 32, 512), BF16),
            pltpu.VMEM((NC, 3, 16, 512), BF16),
            pltpu.VMEM((NC, 3, 16, 512), BF16),
            pltpu.SemaphoreType.DMA((COPIES,)),
            pltpu.SemaphoreType.DMA((COPIES,)),
            pltpu.SemaphoreType.DMA((10 * NC,)),
            pltpu.SemaphoreType.DMA((3 + 2 * NC,)),
        ],
        compiler_params=pltpu.CompilerParams(
            collective_id=0, has_side_effects=True, vmem_limit_bytes=60 * 2**20
        ),
        cost_estimate=pl.CostEstimate(flops=6 * 2**30, bytes_accessed=16 * 2**20, transcendentals=0),
    )(inputs, out_grad, w_in, w_out)
    return weight_grads(
        input_grad, xg.reshape(1024, 512), gg.reshape(1024, 512), act.reshape(1024, 2048), pre_grad.reshape(1024, 2048)
    )


def weight_grads(input_grad, xg, gg, act, pre_grad):
    blocks = 4

    def body(ig, x, g, a, p, ig_out, wi_out, wo_out, X, G, A, PG, WI, WO, isem, osem):
        def cols(b):
            return pl.ds(512 * b, 512)

        def start(src, dst, sem):
            copy = pltpu.make_async_copy(src, dst, sem)
            copy.start()
            return copy

        x_in = start(x, X, isem.at[0])
        p_in = [start(p.at[:, cols(b)], PG.at[b], isem.at[2 + b]) for b in range(blocks)]
        g_in = start(g, G, isem.at[1])
        a_in = [start(a.at[:, cols(b)], A.at[b], isem.at[2 + blocks + b]) for b in range(blocks)]
        outs = [start(ig, ig_out, osem.at[2 * blocks])]
        x_in.wait()
        for b in range(blocks):
            p_in[b].wait()
            WI[b] = lax.dot_general(X[...], PG[b], TN, preferred_element_type=F32)
            outs.append(start(WI.at[b], wi_out.at[:, cols(b)], osem.at[b]))
        g_in.wait()
        for b in range(blocks):
            a_in[b].wait()
            WO[b] = lax.dot_general(A[b], G[...], TN, preferred_element_type=F32)
            outs.append(start(WO.at[b], wo_out.at[cols(b), :], osem.at[blocks + b]))
        for copy in outs:
            copy.wait()

    hbm = pl.BlockSpec(memory_space=pl.ANY)
    return pl.pallas_call(
        body,
        out_shape=(
            jax.ShapeDtypeStruct((64, 512), F32),
            jax.ShapeDtypeStruct((512, 2048), F32),
            jax.ShapeDtypeStruct((2048, 512), F32),
        ),
        in_specs=[hbm] * 5,
        out_specs=(hbm,) * 3,
        scratch_shapes=[
            pltpu.VMEM((1024, 512), BF16),
            pltpu.VMEM((1024, 512), BF16),
            pltpu.VMEM((blocks, 1024, 512), BF16),
            pltpu.VMEM((blocks, 1024, 512), BF16),
            pltpu.VMEM((blocks, 512, 512), F32),
            pltpu.VMEM((blocks, 512, 512), F32),
            pltpu.SemaphoreType.DMA((2 + 2 * blocks,)),
            pltpu.SemaphoreType.DMA((2 * blocks + 1,)),
        ],
        compiler_params=pltpu.CompilerParams(vmem_limit_bytes=60 * 2**20),
        cost_estimate=pl.CostEstimate(flops=4 * 2**30, bytes_accessed=18 * 2**20, transcendentals=0),
    )(input_grad, xg, gg, act, pre_grad)


def solution(mesh):
    return jax.shard_map(
        local,
        mesh=mesh,
        in_specs=(P("hid", "row"), P("hid", "row"), P("row", "hid"), P("hid", "row")),
        out_specs=(P("hid", "row"), P("row", "hid"), P("hid", "row")),
        check_vma=False,
    )
```

```python
import jax
import jax.numpy as jnp
from jax import lax
from jax.experimental import pallas as pl
from jax.experimental.pallas import tpu as pltpu
from jax.sharding import PartitionSpec as P

MESH = pl.DeviceIdType.MESH
F32 = jnp.float32
BF16 = jnp.bfloat16
NC = 4
Q = 2
COPIES = 270
NT = (((1,), (1,)), ((), ()))
TN = (((0,), (0,)), ((), ()))

Z_FIRST = ((1, 0), (3, 1),)
Y_FIRST = ((0, 0), (1, 0), (1, 1),)
ORDER = (
    ("Ax", 0, 0), ("Ag", 0, 0), ("A", 1, 0), ("A", 2, 0), ("B1x", 0, 0), ("B3x", 0, 0),
    ("B2x", 0, 0), ("B1g", 0, 0), ("B3g", 0, 0), ("B2g", 0, 0), ("B2", 1, 0), ("B3", 1, 0),
    ("Dx", 0, 0), ("B1", 1, 0), ("A", 3, 0), ("Ex", 0, 1), ("Dg", 0, 0), ("Ex", 0, 0),
    ("B3", 2, 0), ("B1", 2, 0), ("Eg", 0, 0), ("B2", 2, 0), ("D", 1, 0), ("F0x", 0, 1),
    ("F1x", 0, 1), ("Eg", 0, 1), ("F1x", 0, 0), ("B1", 3, 0), ("F0x", 0, 0), ("E", 1, 1),
    ("B2", 3, 0), ("E", 1, 0), ("F1g", 0, 0), ("D", 2, 0), ("F1g", 0, 1), ("F0g", 0, 1),
    ("B3", 3, 0), ("F0g", 0, 0), ("F1", 1, 1), ("F0", 1, 1), ("E", 2, 1), ("E", 2, 0),
    ("G", 0, 1), ("G", 0, 0), ("D", 3, 0), ("F0", 2, 1), ("G", 1, 1), ("F1", 2, 1),
    ("E", 3, 1), ("E", 3, 0), ("F0", 2, 0), ("F1", 2, 0), ("e", 1, 0), ("H", 1, 1),
    ("H", 0, 0), ("H", 0, 1), ("G", 2, 1), ("Sp", 0, 0), ("F1", 3, 0), ("F0", 3, 0),
    ("Sp", 0, 1), ("G", 2, 0), ("F0", 1, 0), ("Sa", 0, 1), ("F1", 1, 0), ("e", 3, 1),
    ("Sp", 1, 1), ("J0p", 0, 0), ("J1p", 0, 0), ("H", 2, 1), ("Sp", 2, 1), ("Ip", 0, 1),
    ("G", 3, 0), ("H", 2, 0), ("Sp", 2, 0), ("F0", 3, 1), ("Sa", 0, 0), ("H", 1, 0),
    ("Sa", 2, 1), ("F1", 3, 1), ("Sp", 1, 0), ("J1p", 1, 1), ("kp", 0, 0), ("J0p", 1, 1),
    ("Sa", 1, 0), ("Ip", 2, 0), ("H", 3, 0), ("J1p", 0, 1), ("Sp", 3, 0), ("J0p", 0, 1),
    ("H", 3, 1), ("J0p", 1, 0), ("J1p", 1, 0), ("Sp", 3, 1), ("Ip", 2, 1), ("kp", 1, 1),
    ("Kp", 0, 0), ("Sa", 1, 1), ("Ip", 3, 0), ("J0p", 2, 0), ("J1p", 2, 0), ("J0a", 0, 0),
    ("J1a", 0, 0), ("kp", 1, 0), ("Kp", 0, 1), ("L", 0, 0), ("J0p", 2, 1), ("J1p", 2, 1),
    ("Ip", 3, 1), ("Sa", 3, 1), ("L", 0, 1), ("Kp", 1, 1), ("Sa", 2, 0), ("J0p", 3, 0),
    ("Sa", 3, 0), ("J1a", 1, 0), ("J1a", 1, 1), ("Kp", 2, 0), ("J0a", 1, 0), ("J1p", 3, 0),
    ("Ia", 0, 1), ("J0a", 1, 1), ("Kp", 2, 1), ("ka", 0, 0), ("L", 2, 0), ("Kp", 1, 0),
    ("J1p", 3, 1), ("J0p", 3, 1), ("L", 2, 1), ("Ia", 2, 1), ("Ia", 3, 1), ("ka", 1, 0),
    ("L", 1, 0), ("Kp", 3, 0), ("L", 1, 1), ("Kp", 3, 1), ("Ia", 3, 0), ("ka", 1, 1),
    ("Ia", 2, 0), ("J1a", 0, 1), ("L", 3, 0), ("L", 3, 1), ("J0a", 0, 1), ("N", 0, 1),
    ("J0a", 3, 1), ("J1a", 3, 1), ("Ka", 1, 0), ("J1a", 2, 1), ("N", 2, 1), ("Ka", 0, 0),
    ("J0a", 3, 0), ("J0a", 2, 1), ("J1a", 3, 0), ("J1a", 2, 0), ("N", 1, 1), ("J0a", 2, 0),
    ("Ka", 1, 1), ("Q", 1, 0), ("Ka", 3, 1), ("N", 3, 1), ("Ka", 3, 0), ("Ka", 2, 0),
    ("Ka", 2, 1), ("Q", 0, 0), ("Q", 1, 1), ("Ka", 0, 1), ("Q", 3, 1), ("Q", 2, 0),
    ("O", 2, 1), ("Q", 0, 1), ("Q", 3, 0), ("Q", 2, 1), ("O", 1, 1), ("O", 0, 1),
    ("O", 3, 1),
)


def gelu_parts(pre):
    phi = 0.5 * (1.0 + lax.erf(pre * 0.7071067811865476))
    dens = jnp.exp(-0.5 * pre * pre) * 0.3989422804014327
    return (pre * phi, phi + pre * dens)


UP, DOWN = 2.0**50, 2.0**-50
UP_IG, DOWN_IG = 2.0**40, 2.0**-40


def encode(v, up=UP):
    return ((v * up) * (jnp.abs(v) * up)).astype(BF16)


def decode(q, down=DOWN):
    q = q.astype(F32)
    root = jnp.sqrt(jnp.abs(q)) * down
    return jnp.where(q < 0, -root, root)


def kernel(x_ref, g_ref, w_in, w_out, ig_ref, xo, go, ao, po,
           XG, WV, W1, W2, PT, TX, RX, ZT, ZR, ACT, IGP, XT, XR, NX, ZX, ssem, rsem, lsem, wsem):
    r, h = lax.axis_index("row"), lax.axis_index("hid")
    core, zl, y = r % 2, (r // 2) % 2, r // 4
    x, zh = h // 4, h % 4

    def dev(y=y, zl=zl, core=core, x=x, zh=zh):
        return {"row": (y * 2 + zl) * 2 + core, "hid": x * 4 + zh}

    yr, yl, yf = (y + 1) % 4, (y + 3) % 4, (y + 2) % 4
    right, left = dev(y=yr), dev(y=yl)
    partner, zpair = dev(core=1 - core), dev(zl=1 - zl)
    xmate = {j: dev(x=(x + j) % 4) for j in (1, 2, 3)}
    zmate = {j: dev(zh=(zh + j) % 4) for j in (1, 2, 3)}
    behind = {j: (zh + 4 - j) % 4 for j in (0, 1, 2, 3)}

    theirs, ours = pl.multiple_of((1 - core) * 1024, 1024), pl.multiple_of(core * 1024, 1024)
    mine_in = {}
    for c in range(NC):
        for a in range(2):
            mine_in[c, a] = pltpu.make_async_copy(
                (x_ref, g_ref)[a].at[pl.ds(16 * c, 16), :], XG.at[c, a, core, h], wsem.at[3 + 2 * c + a]
            )
            mine_in[c, a].start()
    own = [
        pltpu.make_async_copy(w_in.at[:, pl.ds(ours, 1024)], W1.at[core], wsem.at[0]),
        pltpu.make_async_copy(w_out.at[pl.ds(ours, 1024), :], W2.at[core], wsem.at[1]),
        pltpu.make_async_copy(w_in, WV, wsem.at[2]),
    ]
    for copy in own:
        copy.start()

    barrier = pltpu.get_barrier_semaphore()
    others = [right, left, partner, zpair, *xmate.values(), *zmate.values()]
    for other in others:
        pl.semaphore_signal(barrier, inc=1, device_id=other, device_id_type=MESH)
    pl.semaphore_wait(barrier, len(others))

    copies = {}
    locals_ = []

    def send(key, src, dst, to):
        i = len(copies)
        copy = pltpu.make_async_remote_copy(
            src_ref=src, dst_ref=dst, send_sem=ssem.at[i], recv_sem=rsem.at[i], device_id=to, device_id_type=MESH
        )
        copy.start()
        copies[key] = copy

    def arrived(*keys):
        for key in keys:
            copies[key].wait_recv()

    def keep(src, dst):
        copy = pltpu.make_async_copy(src, dst, lsem.at[len(locals_)])
        copy.start()
        locals_.append(copy)

    arrays = {"": (0, 1), "x": (0,), "g": (1,)}
    span = {"": slice(None), "x": pl.ds(0, 1), "g": pl.ds(1, 1)}

    def versions(c):
        return ("x", "g") if c == 0 else ("",)

    def A(c, u, v):
        for a in arrays[v]:
            mine_in[c, a].wait()
        mine = XG.at[c, span[v], core, h]
        for j in (2, 1, 3):
            send((f"A{j}{v}", c), mine, mine, zmate[j])
        across(0, c, v)

    def across(j, c, v):
        block = XG.at[c, span[v], core, 4 * x + behind[j]]
        for i in (2, 1, 3):
            send((f"B{j}{i}{v}", c), block, block, xmate[i])

    def B(j, c, v):
        arrived((f"A{j}{v}", c))
        across(j, c, v)

    def D(c, u, v):
        arrived(*((f"B{j}{i}{v}", c) for j in range(4) for i in (1, 2, 3)))
        mine = XG.at[c, span[v], core]
        send((f"D{v}", c), mine, mine, partner)
        for a in arrays[v]:
            keep(XG.at[c, a, core], (xo, go)[a].at[c])

    ready = []

    def once(key, wait):
        if key not in ready:
            wait()
        ready.append(key)

    def E(c, u, v):
        for a in arrays[v]:
            once(("w", a), lambda a=a: (arrived(("w_in", "w_out")[a]), own[a].wait()))
        once(("D", c, v), lambda: arrived((f"D{v}", c)))

        @pl.loop(0, 2)
        def _(n):
            cols = pl.ds(pl.multiple_of(n * 256, 256), 256)
            wide = pl.ds(pl.multiple_of(n * 256 + 512 * u, 256), 256)
            if 0 in arrays[v]:
                pre = jnp.dot(XG[c, 0, 0].reshape(256, 512), W1[0, :, wide], preferred_element_type=F32)
                pre += jnp.dot(XG[c, 0, 1].reshape(256, 512), W1[1, :, wide], preferred_element_type=F32)
                PT[c, u, 0, :, :, :, cols] = pre.reshape(4, 2, 32, 256)
            if 1 in arrays[v]:
                hid = lax.dot_general(XG[c, 1, 0].reshape(256, 512), W2[0, wide, :], NT, preferred_element_type=F32)
                hid += lax.dot_general(XG[c, 1, 1].reshape(256, 512), W2[1, wide, :], NT, preferred_element_type=F32)
                PT[c, u, 1, :, :, :, cols] = hid.reshape(4, 2, 32, 256)

        if (c, u) in Z_FIRST:
            for a in range(2):
                ZT[c, u, a] = encode(PT[c, u, a, :, 1 - zl])
            send(("z", c, u), ZT.at[c, u], ZR.at[c, u], zpair)
        else:
            tree(c, u, v)

    def e(c, u):
        arrived(("z", c, u))
        for a in range(2):
            PT[c, u, a, :, zl] = PT[c, u, a, :, zl] + decode(ZR[c, u, a])
        tree(c, u, "")

    def part(c, u, a, piece, half):
        if (c, u) in Z_FIRST:
            return PT.at[c, u, a, piece, zl, pl.ds(16 * half, 16)]
        return PT.at[c, u, a, piece, half]

    def rows_of(c, u):
        return pl.ds(0, 16 if (c, u) in Z_FIRST else 32)

    def tree(c, u, v):
        rows = rows_of(c, u)
        for d, kind, piece, half, to in (
            (0, 0, yf, 0, right), (1, 0, yf, 1, left), (0, 1, yr, 1, right), (1, 1, yl, 0, left),
        ):
            for a in arrays[v]:
                TX[c, u, d, kind, a, rows] = encode(part(c, u, a, piece, half)[...])
            send((f"y{d}{kind}{v}", c, u), TX.at[c, u, d, kind, span[v], rows], RX.at[c, u, d, kind, span[v], rows], to)

    def F(d, c, u, v):
        rows = rows_of(c, u)
        piece, half, to = ((yr, 0, right), (yl, 1, left))[d]
        arrived((f"y{d}0{v}", c, u))
        for a in arrays[v]:
            TX[c, u, d, 2, a, rows] = encode(part(c, u, a, piece, half)[...] + decode(RX[c, u, d, 0, a, rows]))
        send((f"y{d}2{v}", c, u), TX.at[c, u, d, 2, span[v], rows], RX.at[c, u, d, 2, span[v], rows], to)

    def sums(c, u):
        arrived(*((f"y{d}{kind}{v}", c, u) for d in range(2) for kind in (1, 2) for v in versions(c)))

    def own_sum(c, u, a, half):
        rows = rows_of(c, u)
        return (
            part(c, u, a, y, half)[...]
            + decode(RX[c, u, 0, 2 - half, a, rows])
            + decode(RX[c, u, 1, 1 + half, a, rows])
        )

    def G(c, u):
        sums(c, u)
        for a in range(2):
            ZT[c, u, a, 0] = encode(own_sum(c, u, a, 1 - zl))
        send(("z", c, u), ZT.at[c, u, :, 0], ZR.at[c, u, :, 0], zpair)
        for a in range(2):
            PT[c, u, a, y, zl] = own_sum(c, u, a, zl)

    def H(c, u):
        if (c, u) in Z_FIRST:
            sums(c, u)
            for half in range(2):
                rows = pl.ds(16 * half, 16)
                value, slope = gelu_parts(own_sum(c, u, 0, half))
                ACT[c, 0, core, u, y, zl, rows] = value.astype(BF16)
                ACT[c, 1, core, u, y, zl, rows] = (own_sum(c, u, 1, half) * slope).astype(BF16)
        else:
            arrived(("z", c, u))
            value, slope = gelu_parts(PT[c, u, 0, y, zl] + decode(ZR[c, u, 0, 0]))
            hidden = PT[c, u, 1, y, zl] + decode(ZR[c, u, 1, 0])
            ACT[c, 0, core, u, y, zl] = value.astype(BF16)
            ACT[c, 1, core, u, y, zl] = (hidden * slope).astype(BF16)

    def S(a, c, u):
        mine = ACT.at[c, a, core, u, y, zl]
        if (c, u) in Y_FIRST:
            send(("I0", a, c, u), mine, mine, right)
            send(("I1", a, c, u), mine, mine, left)
        else:
            send(("S", a, c, u), mine, mine, zpair)

    def I(a, c, u):
        arrived(("S", a, c, u))
        mine = ACT.at[c, a, core, u, y]
        send(("I0", a, c, u), mine, mine, right)
        send(("I1", a, c, u), mine, mine, left)

    def J(d, a, c, u):
        arrived((f"I{d}", a, c, u))
        piece, to = ((yl, right), (yr, left))[d]
        if (c, u) in Y_FIRST:
            block = ACT.at[c, a, core, u, piece, zl, pl.ds(16 * d, 16)]
        else:
            block = ACT.at[c, a, core, u, piece, d]
        send((f"J{d}", a, c, u), block, block, to)

    def k(a, c, u):
        arrived(("J0", a, c, u), ("J1", a, c, u))
        mine = ACT.at[c, a, core, u, :, zl]
        send(("k", a, c, u), mine, mine, zpair)

    def K(a, c, u):
        arrived(*([("k", a, c, u)] if (c, u) in Y_FIRST else [("J0", a, c, u), ("J1", a, c, u)]))
        mine = ACT.at[c, a, core, u]
        send(("K", a, c, u), mine, mine, partner)

    def whole(a, c, u):
        arrived(("K", a, c, u))
        for half in range(2):
            keep(ACT.at[c, a, half, u], (ao, po)[a].at[2 * half + u, c])

    def L(c, u):
        whole(1, c, u)
        once(("w", 2), own[2].wait)

        @pl.loop(0, 2)
        def _(n):
            rows = pl.ds(pl.multiple_of(n * 256, 256), 256)
            total = jnp.zeros((256, 256), F32)
            for half in range(2):
                total += lax.dot_general(
                    ACT[c, 1, half, u].reshape(256, 512), WV[rows, pl.ds(1024 * half + 512 * u, 512)], NT,
                    preferred_element_type=F32,
                )
            total = total.reshape(4, 2, 32, 256)
            IGP[c, :, :, :, rows] = total if u == 0 else IGP[c, :, :, :, rows] + total

        if u == 0:
            return
        for j in (2, 1, 3):
            XT[c, j - 1] = encode(IGP[c, (x + j) % 4], UP_IG)
            send((f"x{j}", c), XT.at[c, j - 1], XR.at[c, j - 1], xmate[j])

    def N(c, u):
        arrived(("x1", c), ("x2", c), ("x3", c))
        others = decode(XR[c, 0], DOWN_IG) + decode(XR[c, 1], DOWN_IG) + decode(XR[c, 2], DOWN_IG)
        IGP[c, x] = IGP[c, x] + others
        for j in (2, 1, 3):
            NX[c, j - 1] = encode(rows_for(c, (zh + j) % 4), UP_IG)
            send((f"N{j}", c), NX.at[c, j - 1], ZX.at[c, j - 1], zmate[j])

    def rows_for(c, to):
        return IGP[c, x, to // 2, pl.ds(pl.multiple_of((to % 2) * 16, 16), 16)]

    def O(c, u):
        arrived(("N1", c), ("N2", c), ("N3", c))
        others = decode(ZX[c, 0], DOWN_IG) + decode(ZX[c, 1], DOWN_IG) + decode(ZX[c, 2], DOWN_IG)
        ig_ref[pl.ds(16 * c, 16), :] = rows_for(c, zh) + others

    stages = dict(e=e, G=G, H=H, L=L, N=N, O=O, Q=lambda c, u: whole(0, c, u))
    for v in ("", "x", "g"):
        for name, f in (("A", A), ("D", D), ("E", E)):
            stages[name + v] = lambda c, u, f=f, v=v: f(c, u, v)
        for j in (1, 2, 3):
            stages[f"B{j}{v}"] = lambda c, u, j=j, v=v: B(j, c, v)
        for d in range(2):
            stages[f"F{d}{v}"] = lambda c, u, d=d, v=v: F(d, c, u, v)
    for a, v in enumerate("ap"):
        for name, f in (("S", S), ("I", I), ("k", k), ("K", K)):
            stages[name + v] = lambda c, u, a=a, f=f: f(a, c, u)
        for d in range(2):
            stages[f"J{d}{v}"] = lambda c, u, d=d, a=a: J(d, a, c, u)

    for i, (stage, c, u) in enumerate(ORDER):
        stages[stage](c, u)
        if i == 0:
            send("w_in", w_in.at[:, pl.ds(theirs, 1024)], W1.at[core], partner)
            send("w_out", w_out.at[pl.ds(theirs, 1024), :], W2.at[core], partner)
    for copy in copies.values():
        copy.wait_send()
    for copy in locals_:
        copy.wait()


def local(inputs, out_grad, w_in, w_out):
    vmem = pl.BlockSpec(memory_space=pltpu.VMEM)
    hbm = pl.BlockSpec(memory_space=pl.ANY)
    input_grad, xg, gg, act, pre_grad = pl.pallas_call(
        kernel,
        out_shape=(
            jax.ShapeDtypeStruct((64, 512), F32),
            jax.ShapeDtypeStruct((NC, 16, 16, 512), BF16),
            jax.ShapeDtypeStruct((NC, 16, 16, 512), BF16),
            jax.ShapeDtypeStruct((2 * Q, NC, 4, 2, 32, 512), BF16),
            jax.ShapeDtypeStruct((2 * Q, NC, 4, 2, 32, 512), BF16),
        ),
        in_specs=[hbm] * 4,
        out_specs=(vmem, hbm, hbm, hbm, hbm),
        scratch_shapes=[
            pltpu.VMEM((NC, 2, 2, 16, 16, 512), BF16),
            pltpu.VMEM((512, 2048), BF16),
            pltpu.VMEM((2, 512, 1024), BF16),
            pltpu.VMEM((2, 1024, 512), BF16),
            pltpu.VMEM((NC, Q, 2, 4, 2, 32, 512), F32),
            pltpu.VMEM((NC, Q, 2, 3, 2, 32, 512), BF16),
            pltpu.VMEM((NC, Q, 2, 3, 2, 32, 512), BF16),
            pltpu.VMEM((NC, Q, 2, 4, 32, 512), BF16),
            pltpu.VMEM((NC, Q, 2, 4, 32, 512), BF16),
            pltpu.VMEM((NC, 2, 2, Q, 4, 2, 32, 512), BF16),
            pltpu.VMEM((NC, 4, 2, 32, 512), F32),
            pltpu.VMEM((NC, 3, 2, 32, 512), BF16),
            pltpu.VMEM((NC, 3, 2, 32, 512), BF16),
            pltpu.VMEM((NC, 3, 16, 512), BF16),
            pltpu.VMEM((NC, 3, 16, 512), BF16),
            pltpu.SemaphoreType.DMA((COPIES,)),
            pltpu.SemaphoreType.DMA((COPIES,)),
            pltpu.SemaphoreType.DMA((10 * NC,)),
            pltpu.SemaphoreType.DMA((3 + 2 * NC,)),
        ],
        compiler_params=pltpu.CompilerParams(
            collective_id=0, has_side_effects=True, vmem_limit_bytes=60 * 2**20
        ),
        cost_estimate=pl.CostEstimate(flops=6 * 2**30, bytes_accessed=16 * 2**20, transcendentals=0),
    )(inputs, out_grad, w_in, w_out)
    return weight_grads(
        input_grad, xg.reshape(1024, 512), gg.reshape(1024, 512), act.reshape(4, 1024, 512), pre_grad.reshape(4, 1024, 512)
    )


def weight_grads(input_grad, xg, gg, act, pre_grad):
    blocks = 4

    def body(ig, x, g, a, p, ig_out, wi_out, wo_out, X, G, A, PG, WI, WO, isem, osem):
        def cols(b):
            return pl.ds(512 * b, 512)

        def start(src, dst, sem):
            copy = pltpu.make_async_copy(src, dst, sem)
            copy.start()
            return copy

        x_in = start(x, X, isem.at[0])
        p_in = [start(p.at[b], PG.at[b], isem.at[2 + b]) for b in range(blocks)]
        g_in = start(g, G, isem.at[1])
        a_in = [start(a.at[b], A.at[b], isem.at[2 + blocks + b]) for b in range(blocks)]
        outs = [start(ig, ig_out, osem.at[2 * blocks])]
        x_in.wait()
        for b in range(blocks):
            p_in[b].wait()
            WI[b] = lax.dot_general(X[...], PG[b], TN, preferred_element_type=F32)
            outs.append(start(WI.at[b], wi_out.at[:, cols(b)], osem.at[b]))
        g_in.wait()
        for b in range(blocks):
            a_in[b].wait()
            WO[b] = lax.dot_general(A[b], G[...], TN, preferred_element_type=F32)
            outs.append(start(WO.at[b], wo_out.at[cols(b), :], osem.at[blocks + b]))
        for copy in outs:
            copy.wait()

    hbm = pl.BlockSpec(memory_space=pl.ANY)
    return pl.pallas_call(
        body,
        out_shape=(
            jax.ShapeDtypeStruct((64, 512), F32),
            jax.ShapeDtypeStruct((512, 2048), F32),
            jax.ShapeDtypeStruct((2048, 512), F32),
        ),
        in_specs=[hbm] * 5,
        out_specs=(hbm,) * 3,
        scratch_shapes=[
            pltpu.VMEM((1024, 512), BF16),
            pltpu.VMEM((1024, 512), BF16),
            pltpu.VMEM((blocks, 1024, 512), BF16),
            pltpu.VMEM((blocks, 1024, 512), BF16),
            pltpu.VMEM((blocks, 512, 512), F32),
            pltpu.VMEM((blocks, 512, 512), F32),
            pltpu.SemaphoreType.DMA((2 + 2 * blocks,)),
            pltpu.SemaphoreType.DMA((2 * blocks + 1,)),
        ],
        compiler_params=pltpu.CompilerParams(vmem_limit_bytes=60 * 2**20),
        cost_estimate=pl.CostEstimate(flops=4 * 2**30, bytes_accessed=18 * 2**20, transcendentals=0),
    )(input_grad, xg, gg, act, pre_grad)


def solution(mesh):
    return jax.shard_map(
        local,
        mesh=mesh,
        in_specs=(P("hid", "row"), P("hid", "row"), P("row", "hid"), P("hid", "row")),
        out_specs=(P("hid", "row"), P("row", "hid"), P("hid", "row")),
        check_vma=False,
    )
```
